32 devices in a mesh: group: 2 (over x), freq: 16 (over z, y, core).
Axes of the slice: x: 2, y: 2, z: 4, core: 2. Of those that a mesh axis runs over, the one named last changes fastest.
Arguments:
- slip_history: float32 [512, 3, 16384], P('freq', None, 'group'), parts along dimension 2, may hold values from -6 to 6
- frequency_ids: int32 [16], replicated, may hold values from 0 to 256, as said below
- col_clusters: int32 [64, 8], replicated, may hold values from 0 to 63, as said below
- basis_ranks: int32 [16, 128], P('freq', 'group'), parts along dimension 1, may hold values from 8 to 32
- left_basis: bfloat16 [16, 128, 2, 32, 3, 128], P('freq', 'group'), parts along dimension 1, may hold values from -0.75 to 0.75
- right_basis: bfloat16 [16, 128, 2, 32, 3, 128], P('freq', 'group'), parts along dimension 1, may hold values from -0.21875 to 0.21875
- coupling: bfloat16 [16, 128, 8, 2, 1024], P('freq', 'group'), parts along dimension 1, may hold values from -0.25 to 0.25
Outputs:
- traction: float32 [512, 3, 16384], P('freq', None, 'group'), parts along dimension 2
The draws below stay inside these ranges and needn't reach their ends.
There are 2 independent parts, one for each index of `group`. The reference program is written for one: setup_inputs(seed, part) draws one part's arguments, and reference() takes and returns one part's arrays. A program takes and returns all parts, laid end to end along the dimension named above; an argument that names none is the same for every part. Nothing has to cross between parts.
Inputs may be any that keep to these rules, and one draw needn't show every extreme that they name: `frequency_ids`: distinct frequency numbers; 0 and 256 are always among them. `col_clusters`: each row a lists 8 distinct clusters, the first of them a itself.
All inputs are finite; a program needn't handle non-finite values.
Results may differ from the reference program's by a relative error of at most 0.0057.
Values may be sent and summed in bfloat16 or wider, within the bound.
A program may use at most 128 MiB of HBM per device.

```python
import math
import jax
import jax.numpy as jnp
from jax import lax

STEPS = 512
LEAF = 128
RANK = 32
BLOCKS = 8
ELEMENTS = 8192
FREQ = 16
CLUSTERS = 64


def draw_frequency_ids(key, part):
    key = jax.random.fold_in(key, 11)
    interior = jax.random.permutation(key, STEPS // 2 - 1)[:FREQ - 2] + 1
    end_points = jnp.array([0, STEPS // 2], dtype=jnp.int32)
    chosen = jnp.concatenate([end_points, interior.astype(jnp.int32)])
    return jax.random.permutation(jax.random.fold_in(key, 1), chosen).astype(jnp.int32)


def pick_offsets(subkey):
    return jax.random.permutation(subkey, ELEMENTS // LEAF - 1)[:BLOCKS - 1]


def draw_col_clusters(key, part):
    key = jax.random.fold_in(key, 23)
    clusters = ELEMENTS // LEAF
    subkeys = jax.random.split(key, clusters)
    offsets = jax.vmap(pick_offsets)(subkeys).astype(jnp.int32) + 1
    row_ids = jnp.arange(clusters, dtype=jnp.int32)[:, None]
    others = (row_ids + offsets) % clusters
    return jnp.concatenate([row_ids, others], axis=1).astype(jnp.int32)


def draw_basis_ranks(key, part):
    key = jax.random.fold_in(key, 37)
    drawn = jax.random.randint(key, (FREQ, ELEMENTS // LEAF), RANK // 4, RANK + 1, dtype=jnp.int32)
    drawn = drawn.at[:, 0].set(RANK)
    return drawn.at[:, 1].set(RANK // 4)


def shard_levels(key, dims, pieces, least, top_value):
    gain, own = 1.0, jax.random.fold_in(key, 6)
    for position, parts in pieces:
        steps = jnp.exp(jax.random.uniform(jax.random.fold_in(own, position), (parts,), jnp.float32, least / len(pieces), top_value / len(pieces)))
        gain = gain * jnp.repeat(steps, dims[position] // parts).reshape([-1 if axis == position else 1 for axis in range(len(dims))])
    return gain


def normal_values(own_key, dims, spread, bound, cuts=(), held_as=jnp.bfloat16):
    factor_of = shard_levels(own_key, dims, cuts, -0.22, 0.18) if cuts else 1.0
    values = jax.random.normal(own_key, dims, jnp.float32) * spread * factor_of
    return jnp.minimum(jnp.maximum(values, -bound), bound).astype(held_as)


def setup_inputs(seed: int = 0, part: int = 0) -> dict:
    arg_keys = jax.random.split(jax.random.key(seed), 8)
    part_keys = jax.random.split(jax.random.fold_in(arg_keys[7], part), 8)
    return {
        "slip_history": normal_values(part_keys[0], (STEPS, 3, ELEMENTS), 1.0, 6.0, ((0, 16),), jnp.float32),
        "frequency_ids": draw_frequency_ids(jax.random.fold_in(arg_keys[7], 71), part),
        "col_clusters": draw_col_clusters(jax.random.fold_in(arg_keys[7], 71), part),
        "basis_ranks": draw_basis_ranks(jax.random.fold_in(jax.random.fold_in(arg_keys[7], part), 71), part),
        "left_basis": normal_values(part_keys[4], (FREQ, CLUSTERS, 2, RANK, 3, LEAF), (2 * RANK) ** -0.5, 0.75, ((0, 16),)),
        "right_basis": normal_values(part_keys[5], (FREQ, CLUSTERS, 2, RANK, 3, LEAF), (6 * LEAF) ** -0.5, 0.21875, ((0, 16),)),
        "coupling": normal_values(part_keys[6], (FREQ, CLUSTERS, BLOCKS, 2, RANK * RANK), (2 * RANK * BLOCKS) ** -0.5, 0.25, ((0, 16),)),
    }


DAMPING = 0.5


def forward_table(frequency_ids, time_ids):
    phases = (frequency_ids[:, None] * time_ids[None, :]) % STEPS
    angles = phases.astype(jnp.float32) * (2.0 * math.pi / STEPS)
    weights = DAMPING ** (time_ids.astype(jnp.float32) / STEPS)
    return jnp.stack([weights[None, :] * jnp.cos(angles), -weights[None, :] * jnp.sin(angles)])


def inverse_table(frequency_ids, time_ids):
    phases = (time_ids[:, None] * frequency_ids[None, :]) % STEPS
    angles = phases.astype(jnp.float32) * (2.0 * math.pi / STEPS)
    scales = DAMPING ** (-time_ids.astype(jnp.float32) / STEPS) / STEPS
    doubled = jnp.where((frequency_ids == 0) | (frequency_ids == STEPS // 2), 1.0, 2.0)
    factor = scales[:, None] * doubled[None, :]
    return jnp.stack([factor * jnp.cos(angles), -factor * jnp.sin(angles)], axis=1)


def apply_operator(spectrum, right_part, left_part, coupling, rank_row, col_clusters):
    clusters = right_part.shape[0]
    rank_ids = jnp.arange(right_part.shape[2], dtype=jnp.int32)
    kept_mask = (rank_ids[None, :] < rank_row[:, None]).astype(jnp.float32)[:, None, :]
    products = jnp.einsum("pjnc,nqkjc->npqk", spectrum.astype(jnp.float32), right_part.astype(jnp.float32))
    real_part = products[:, 0, 0] - products[:, 1, 1]
    imag_part = products[:, 1, 0] + products[:, 0, 1]
    coeffs = (jnp.stack([real_part, imag_part], axis=1) * kept_mask).astype(jnp.bfloat16)
    gathered = coeffs[col_clusters]
    blocks = coupling.reshape(clusters, coupling.shape[1], 2, right_part.shape[2], right_part.shape[2])
    coupled = jnp.einsum("nbqkl,nbpl->npqk", blocks.astype(jnp.float32), gathered.astype(jnp.float32))
    real_part = coupled[:, 0, 0] - coupled[:, 1, 1]
    imag_part = coupled[:, 1, 0] + coupled[:, 0, 1]
    middle = (jnp.stack([real_part, imag_part], axis=1) * kept_mask).astype(jnp.bfloat16)
    images = jnp.einsum("npk,nqkjc->npqjc", middle.astype(jnp.float32), left_part.astype(jnp.float32))
    real_part = images[:, 0, 0] - images[:, 1, 1]
    imag_part = images[:, 1, 0] + images[:, 0, 1]
    result = jnp.stack([real_part, imag_part])
    return jnp.transpose(result, (0, 2, 1, 3)).astype(jnp.bfloat16)


def reference(slip_history, frequency_ids, col_clusters, basis_ranks, left_basis, right_basis, coupling):
    time_ids = jnp.arange(STEPS, dtype=jnp.int32)
    forward_rows = forward_table(frequency_ids, time_ids).reshape(2 * FREQ, STEPS)
    flattened = slip_history.reshape(STEPS, 3 * ELEMENTS)
    spectra = jnp.dot(forward_rows, flattened, precision=lax.Precision.HIGHEST, preferred_element_type=jnp.float32)
    spectra = spectra.reshape(2, FREQ, 3, CLUSTERS, LEAF).astype(jnp.bfloat16)

    def one_frequency(operands):
        spectrum, right_part, left_part, blocks, rank_row = operands
        return apply_operator(spectrum, right_part, left_part, blocks, rank_row, col_clusters)

    images = lax.map(one_frequency, (jnp.moveaxis(spectra, 1, 0), right_basis, left_basis, coupling, basis_ranks))
    images = jnp.moveaxis(images, 0, 1).reshape(2 * FREQ, 3 * ELEMENTS)
    inverse_rows = inverse_table(frequency_ids, time_ids).reshape(STEPS, 2 * FREQ)
    traction = jnp.dot(inverse_rows, images.astype(jnp.float32), precision=lax.Precision.HIGHEST, preferred_element_type=jnp.float32)
    return traction.reshape(STEPS, 3, ELEMENTS)
```

```python
import functools
import math

import jax
import jax.numpy as jnp
from jax import lax
from jax.experimental import pallas as pl
from jax.experimental.pallas import tpu as pltpu
from jax.sharding import PartitionSpec as P

STEPS = 512
DAMPING = 0.5
LEAF = 128
CHUNKS = 8
MESH = pl.DeviceIdType.MESH
MIB = 1024 * 1024


def split_f32(x):
    hi = x.astype(jnp.bfloat16)
    lo = (x - hi.astype(jnp.float32)).astype(jnp.bfloat16)
    return hi, lo


def forward_matrix(frequency_ids, time_ids):
    phases = frequency_ids[:, None] * time_ids[None, :] % STEPS
    angles = phases.astype(jnp.float32) * (2.0 * math.pi / STEPS)
    weights = DAMPING ** (time_ids.astype(jnp.float32) / STEPS)
    table = jnp.stack([weights[None, :] * jnp.cos(angles), -weights[None, :] * jnp.sin(angles)], axis=1)
    hi, lo = split_f32(table)
    eye = jnp.eye(CHUNKS, dtype=jnp.bfloat16)
    rows = table.shape[0] * 2 * CHUNKS
    spread = lambda part: (part[:, :, None, None, :] * eye[None, None, :, :, None]).reshape(rows, -1)
    return jnp.concatenate([spread(hi), spread(hi), spread(lo)], axis=1)


def inverse_matrix(frequency_ids, time_ids):
    phases = time_ids[:, None] * frequency_ids[None, :] % STEPS
    angles = phases.astype(jnp.float32) * (2.0 * math.pi / STEPS)
    scales = DAMPING ** (-time_ids.astype(jnp.float32) / STEPS) / STEPS
    doubled = jnp.where((frequency_ids == 0) | (frequency_ids == STEPS // 2), 1.0, 2.0)
    factor = scales[:, None] * doubled[None, :]
    table = jnp.stack([factor * jnp.cos(angles), -factor * jnp.sin(angles)], axis=2)
    hi, lo = split_f32(table)
    eye = jnp.eye(CHUNKS, dtype=jnp.bfloat16)
    rows = table.shape[0] * CHUNKS
    spread = lambda part: (part[None, :, :, :, None] * eye[:, None, None, None, :]).reshape(rows, -1)
    return spread(hi), spread(lo)


def place(zs, ys):
    me = lax.axis_index("freq")
    core = lax.rem(me, 2)
    y = lax.rem(me // 2, ys)
    z = me // (2 * ys)
    return z, y, core


def index_of(z, y, core, ys):
    return (z * ys + y) * 2 + core


def greet(targets):
    barrier = pltpu.get_barrier_semaphore()
    for target in targets:
        pl.semaphore_signal(barrier, inc=1, device_id={"freq": target}, device_id_type=MESH)
    return lambda: pl.semaphore_wait(barrier, len(targets))


def partners(z, y, core, zs, ys):
    targets = [index_of(z, y, 1 - core, ys)]
    targets += [index_of(z, lax.rem(y + s, ys), core, ys) for s in range(1, ys)]
    targets += [index_of(lax.rem(z + s, zs), y, core, ys) for s in range(1, zs)]
    return targets


def scatter_kernel(zs, ys, table_ref, slip_ref, out_ref, acc, send0, recv0, send1, recv1, send2, recv2, *sems):
    ss0, rs0, ss1, rs1, ss2, rs2 = sems
    z, y, core = place(zs, ys)
    ready = greet(partners(z, y, core, zs, ys))
    times, width = slip_ref.shape[1], slip_ref.shape[2] // CHUNKS
    order = list(range(zs // 2, zs // 2 - zs, -1))
    order = [s % zs for s in order if s % zs] + [0]
    for j in range(3):
        x = jnp.concatenate([slip_ref[j, :, c * width:(c + 1) * width] for c in range(CHUNKS)], axis=0)
        hi, lo = split_f32(x)
        stack = jnp.concatenate([hi, lo, hi], axis=0)
        res = jnp.dot(table_ref[...], stack, preferred_element_type=jnp.float32)
        res = res.reshape(zs * ys, 2, 2 * CHUNKS, width)
        first, second = res[:, 0], res[:, 1]
        own = jnp.where(core == 0, first, second)
        other = jnp.where(core == 0, second, first)
        acc[:, j] = own
        send0[:, j] = other.astype(jnp.bfloat16)
    ready()
    stage0 = {}
    for s in order:
        at = lax.rem(z + s, zs)
        rows = pl.ds(at * ys, ys)
        stage0[s] = pltpu.make_async_remote_copy(
            src_ref=send0.at[rows], dst_ref=recv0.at[rows], send_sem=ss0.at[s], recv_sem=rs0.at[s],
            device_id={"freq": index_of(z, y, 1 - core, ys)}, device_id_type=MESH)
        stage0[s].start()
    stage1, stage2 = {}, {}
    for s in order:
        at = lax.rem(z + s, zs)
        stage0[s].wait_recv()
        for step in range(1, ys):
            there = lax.rem(y + step, ys)
            block = at * ys + there
            send1[step - 1, at] = (acc[block] + recv0[block].astype(jnp.float32)).astype(jnp.bfloat16)
            stage1[s, step] = pltpu.make_async_remote_copy(
                src_ref=send1.at[step - 1, at], dst_ref=recv1.at[step - 1, at],
                send_sem=ss1.at[step - 1, s], recv_sem=rs1.at[step - 1, s],
                device_id={"freq": index_of(z, there, core, ys)}, device_id_type=MESH)
            stage1[s, step].start()
    for s in order:
        at = lax.rem(z + s, zs)
        block = at * ys + y
        total = acc[block] + recv0[block].astype(jnp.float32)
        for step in range(1, ys):
            stage1[s, step].wait_recv()
            total += recv1[step - 1, at].astype(jnp.float32)
        if s:
            send2[s - 1] = total.astype(jnp.bfloat16)
            stage2[s] = pltpu.make_async_remote_copy(
                src_ref=send2.at[s - 1], dst_ref=recv2.at[s - 1], send_sem=ss2.at[s - 1], recv_sem=rs2.at[s - 1],
                device_id={"freq": index_of(at, y, core, ys)}, device_id_type=MESH)
            stage2[s].start()
    for s in order[:-1]:
        stage2[s].wait_recv()
        total += recv2[s - 1].astype(jnp.float32)
    out_ref[...] = total.astype(jnp.bfloat16)
    for copies in (stage0, stage1, stage2):
        for copy in copies.values():
            copy.wait_send()


def scatter_spectra(table, slip, zs, ys):
    block = (3, 2 * CHUNKS, slip.shape[2] // CHUNKS)
    bf16 = jnp.bfloat16
    high, many = max(ys - 1, 1), max(zs - 1, 1)
    return pl.pallas_call(
        functools.partial(scatter_kernel, zs, ys),
        out_shape=jax.ShapeDtypeStruct(block, bf16),
        in_specs=[pl.BlockSpec(memory_space=pltpu.VMEM)] * 2,
        out_specs=pl.BlockSpec(memory_space=pltpu.VMEM),
        scratch_shapes=[
            pltpu.VMEM((zs * ys,) + block, jnp.float32),
            pltpu.VMEM((zs * ys,) + block, bf16),
            pltpu.VMEM((zs * ys,) + block, bf16),
            pltpu.VMEM((high, zs) + block, bf16),
            pltpu.VMEM((high, zs) + block, bf16),
            pltpu.VMEM((many,) + block, bf16),
            pltpu.VMEM((many,) + block, bf16),
            pltpu.SemaphoreType.DMA((zs,)),
            pltpu.SemaphoreType.DMA((zs,)),
            pltpu.SemaphoreType.DMA((high, zs)),
            pltpu.SemaphoreType.DMA((high, zs)),
            pltpu.SemaphoreType.DMA((many,)),
            pltpu.SemaphoreType.DMA((many,)),
        ],
        compiler_params=pltpu.CompilerParams(collective_id=0, has_side_effects=True, vmem_limit_bytes=48 * MIB),
        name="spectra_scatter",
    )(table, slip)


def operator_kernel(spec_ref, right_ref, coupling_ref, left_ref, rank_ref, col_ref, image_ref, coef, tiled, sums):
    f32, bf16 = jnp.float32, jnp.bfloat16
    groups = spec_ref.shape[2] // LEAF
    rank = right_ref.shape[3]
    clusters = groups * CHUNKS
    blocks = coupling_ref.shape[1]
    chunk_row = lax.broadcasted_iota(jnp.int32, (2 * CHUNKS, 2 * rank), 0) % CHUNKS
    half = CHUNKS // 2
    for g in range(groups):
        lanes = slice(g * LEAF, (g + 1) * LEAF)
        x = jnp.concatenate([spec_ref[j, :, lanes] for j in range(3)], axis=1)
        prod = jnp.zeros((2 * CHUNKS, 2 * rank), f32)
        for h in range(2):
            basis = jnp.concatenate(
                [jnp.concatenate([right_ref[(h * half + c) * groups + g, q, j] for c in range(half) for q in range(2)], axis=0)
                 for j in range(3)], axis=1)
            full = lax.dot_general(x, basis, (((1,), (1,)), ((), ())), preferred_element_type=f32)
            for c in range(half):
                prod = jnp.where(chunk_row == h * half + c, full[:, c * 2 * rank:(c + 1) * 2 * rank], prod)
        low, high = prod[:CHUNKS], prod[CHUNKS:]
        rows = slice(g * CHUNKS, (g + 1) * CHUNKS)
        coef[0, rows] = low[:, :rank] - high[:, rank:]
        coef[1, rows] = high[:, :rank] + low[:, rank:]
    kept = lax.broadcasted_iota(jnp.int32, (clusters, rank), 1) < rank_ref[...]
    area = rank * rank
    lane_of = lax.broadcasted_iota(jnp.int32, (rank, area), 1)
    spread = (lane_of % rank == lax.broadcasted_iota(jnp.int32, (rank, area), 0)).astype(bf16)
    for p in range(2):
        held = jnp.where(kept, coef[p], 0.0).astype(bf16)
        tiled[p] = jnp.dot(held, spread, preferred_element_type=f32)

    def couple(step, carry):
        found = [[], []]
        for r in range(4):
            a = step * 4 + r
            totals = [jnp.zeros((2, area), f32), jnp.zeros((2, area), f32)]
            for i in range(blocks):
                source = col_ref[a, i]
                row = (source % groups) * CHUNKS + source // groups
                block = coupling_ref[a, i].astype(f32)
                for p in range(2):
                    totals[p] = totals[p] + block * tiled[p, pl.ds(row, 1), :]
            found[0].append(totals[0])
            found[1].append(totals[1])
        for p in range(2):
            sums[p, pl.ds(pl.multiple_of(step * 8, 8), 8), :] = jnp.concatenate(found[p], axis=0)
        return carry

    lax.fori_loop(0, clusters // 4, couple, 0)
    row_of = lax.broadcasted_iota(jnp.int32, (area, rank), 0)
    gather = (row_of // rank == lax.broadcasted_iota(jnp.int32, (area, rank), 1)).astype(bf16)
    target = lax.broadcasted_iota(jnp.int32, (clusters, 2 * clusters), 0)
    origin = lax.broadcasted_iota(jnp.int32, (clusters, 2 * clusters), 1)
    cluster = (target % CHUNKS) * groups + target // CHUNKS
    picks = [(origin == 2 * cluster + q).astype(f32) for q in range(2)]
    parts = {}
    for p in range(2):
        hi, lo = split_f32(sums[p])
        short = jnp.dot(hi, gather, preferred_element_type=f32) + jnp.dot(lo, gather, preferred_element_type=f32)
        for q in range(2):
            parts[p, q] = jnp.dot(picks[q], short, precision=lax.Precision.HIGHEST, preferred_element_type=f32)
    real = jnp.where(kept, parts[0, 0] - parts[1, 1], 0.0)
    imag = jnp.where(kept, parts[1, 0] + parts[0, 1], 0.0)
    for g in range(groups):
        rows = slice(g * CHUNKS, (g + 1) * CHUNKS)
        mixed = jnp.concatenate([
            jnp.concatenate([real[rows], -imag[rows]], axis=1),
            jnp.concatenate([imag[rows], real[rows]], axis=1)], axis=0)
        masked = jnp.concatenate([jnp.where(chunk_row == c, mixed, 0.0) for c in range(CHUNKS)], axis=1).astype(bf16)
        for j in range(3):
            basis = jnp.concatenate([left_ref[c * groups + g, q, j] for c in range(CHUNKS) for q in range(2)], axis=0)
            out = jnp.dot(masked, basis, preferred_element_type=f32)
            image_ref[j, :, g * LEAF:(g + 1) * LEAF] = out.astype(bf16)


def apply_operator(spectrum, right, coupling, left, ranks, col_clusters):
    clusters, rank = right.shape[0], right.shape[3]
    groups = clusters // CHUNKS
    order = ranks.reshape(CHUNKS, groups).T.reshape(clusters, 1)
    vmem = pl.BlockSpec(memory_space=pltpu.VMEM)
    return pl.pallas_call(
        operator_kernel,
        out_shape=jax.ShapeDtypeStruct(spectrum.shape, jnp.bfloat16),
        in_specs=[vmem] * 5 + [pl.BlockSpec(memory_space=pltpu.SMEM)],
        out_specs=vmem,
        scratch_shapes=[
            pltpu.VMEM((2, clusters, rank), jnp.float32),
            pltpu.VMEM((2, clusters, rank * rank), jnp.float32),
            pltpu.VMEM((2, 2 * clusters, rank * rank), jnp.float32),
        ],
        compiler_params=pltpu.CompilerParams(vmem_limit_bytes=40 * MIB),
        name="operator",
    )(spectrum, right, coupling, left, order, col_clusters)


def gather_kernel(zs, ys, image_ref, out_ref, local_sem, *sems):
    zsend, zrecv, ysend, yrecv, csend, crecv = sems
    z, y, core = place(zs, ys)
    ready = greet(partners(z, y, core, zs, ys))
    me = index_of(z, y, core, ys)
    mine = pltpu.make_async_copy(image_ref, out_ref.at[me], local_sem)
    mine.start()
    ready()
    copies = []

    def send(block, source, target, send_sem, recv_sem):
        copy = pltpu.make_async_remote_copy(
            src_ref=source, dst_ref=out_ref.at[block], send_sem=send_sem, recv_sem=recv_sem,
            device_id={"freq": target}, device_id_type=MESH)
        copy.start()
        copies.append(copy)
        return copy

    other = index_of(z, y, 1 - core, ys)
    order = [s % zs for s in range(zs // 2, zs // 2 - zs, -1) if s % zs]
    for s in order:
        send(me, image_ref, index_of(lax.rem(z + s, zs), y, core, ys), zsend.at[s - 1], zrecv.at[s - 1])
    for step in range(1, ys):
        send(me, image_ref, index_of(z, lax.rem(y + step, ys), core, ys), ysend.at[step - 1, 0], yrecv.at[step - 1, 0])
    send(me, image_ref, other, csend.at[0, 0], crecv.at[0, 0])

    def arrived(block, recv_sem):
        pltpu.make_async_copy(out_ref.at[block], out_ref.at[block], recv_sem).wait()

    near = sorted(range(1, zs), key=lambda s: min(s, zs - s))
    for s in near:
        block = index_of(lax.rem(z + zs - s, zs), y, core, ys)
        arrived(block, zrecv.at[s - 1])
        for step in range(1, ys):
            send(block, out_ref.at[block], index_of(z, lax.rem(y + step, ys), core, ys),
                 ysend.at[step - 1, s], yrecv.at[step - 1, s])
        send(block, out_ref.at[block], other, csend.at[0, s], crecv.at[0, s])
    for s in [0] + near:
        for step in range(1, ys):
            block = index_of(lax.rem(z + zs - s, zs), lax.rem(y + ys - step, ys), core, ys)
            arrived(block, yrecv.at[step - 1, s])
            send(block, out_ref.at[block], other, csend.at[step, s], crecv.at[step, s])
    for s in [0] + near:
        for step in range(ys):
            block = index_of(lax.rem(z + zs - s, zs), lax.rem(y + ys - step, ys), 1 - core, ys)
            arrived(block, crecv.at[step, s])
    mine.wait()
    for copy in copies:
        copy.wait_send()


def gather_images(image, zs, ys):
    high, many = max(ys - 1, 1), max(zs - 1, 1)
    vmem = pl.BlockSpec(memory_space=pltpu.VMEM)
    return pl.pallas_call(
        functools.partial(gather_kernel, zs, ys),
        out_shape=jax.ShapeDtypeStruct((zs * ys * 2,) + image.shape, image.dtype),
        in_specs=[vmem],
        out_specs=vmem,
        scratch_shapes=[
            pltpu.SemaphoreType.DMA,
            pltpu.SemaphoreType.DMA((many,)),
            pltpu.SemaphoreType.DMA((many,)),
            pltpu.SemaphoreType.DMA((high, zs)),
            pltpu.SemaphoreType.DMA((high, zs)),
            pltpu.SemaphoreType.DMA((ys, zs)),
            pltpu.SemaphoreType.DMA((ys, zs)),
        ],
        compiler_params=pltpu.CompilerParams(collective_id=1, has_side_effects=True, vmem_limit_bytes=32 * MIB),
        name="image_gather",
    )(image)


def synthesis_kernel(hi_ref, lo_ref, image_ref, out_ref):
    width, times = image_ref.shape[2], out_ref.shape[1]
    x = image_ref[...].reshape(-1, width)
    res = jnp.dot(hi_ref[...], x, preferred_element_type=jnp.float32)
    res += jnp.dot(lo_ref[...], x, preferred_element_type=jnp.float32)
    for c in range(CHUNKS):
        out_ref[0, :, c * width:(c + 1) * width] = res[c * times:(c + 1) * times]


def synthesize(hi, lo, images, times):
    n, _, rows, width = images.shape
    whole = pl.BlockSpec(hi.shape, lambda j: (0, 0))
    return pl.pallas_call(
        synthesis_kernel,
        grid=(3,),
        out_shape=jax.ShapeDtypeStruct((3, times, CHUNKS * width), jnp.float32),
        in_specs=[whole, whole, pl.BlockSpec((n, None, rows, width), lambda j: (0, j, 0, 0))],
        out_specs=pl.BlockSpec((1, times, CHUNKS * width), lambda j: (j, 0, 0)),
        compiler_params=pltpu.CompilerParams(vmem_limit_bytes=32 * MIB),
        name="synthesis",
    )(hi, lo, images)


def body(zs, ys, slip_history, frequency_ids, col_clusters, basis_ranks, left_basis, right_basis, coupling):
    times = slip_history.shape[0]
    time_ids = lax.axis_index("freq") * times + jnp.arange(times, dtype=jnp.int32)
    slip = jnp.transpose(slip_history, (1, 0, 2))
    right = jnp.transpose(right_basis[0], (0, 1, 3, 2, 4))
    left = jnp.transpose(left_basis[0], (0, 1, 3, 2, 4))
    spectrum = scatter_spectra(forward_matrix(frequency_ids, time_ids), slip, zs, ys)
    image = apply_operator(spectrum, right, coupling[0], left, basis_ranks[0], col_clusters)
    images = gather_images(image, zs, ys)
    hi, lo = inverse_matrix(frequency_ids, time_ids)
    traction = synthesize(hi, lo, images, times)
    return jnp.transpose(traction, (1, 0, 2))


def solution(mesh):
    ys = max(4 // mesh.shape["group"], 1)
    zs = mesh.shape["freq"] // (2 * ys)
    return jax.shard_map(
        functools.partial(body, zs, ys),
        mesh=mesh,
        in_specs=(
            P("freq", None, "group"),
            P(),
            P(),
            P("freq", "group"),
            P("freq", "group", None, None, None, None),
            P("freq", "group", None, None, None, None),
            P("freq", "group", None, None, None),
        ),
        out_specs=P("freq", None, "group"),
        check_vma=False,
    )
```

```python
import functools
import math

import jax
import jax.numpy as jnp
from jax import lax
from jax.experimental import pallas as pl
from jax.experimental.pallas import tpu as pltpu
from jax.sharding import PartitionSpec as P

STEPS = 512
DAMPING = 0.5
LEAF = 128
CHUNKS = 8
MESH = pl.DeviceIdType.MESH
MIB = 1024 * 1024


def split_f32(x):
    hi = x.astype(jnp.bfloat16)
    lo = (x - hi.astype(jnp.float32)).astype(jnp.bfloat16)
    return hi, lo


def iota(shape, axis):
    return lax.broadcasted_iota(jnp.int32, shape, axis)


def angles_of(frequencies, times):
    phases = (frequencies * times) & (STEPS - 1)
    return phases.astype(jnp.float32) * (2.0 * math.pi / STEPS)


def forward_matrix(ids, first_time, times):
    n = ids.shape[1]
    lanes, rows = CHUNKS * times, n * 2 * CHUNKS
    column = jnp.sum(jnp.where(iota((n, n), 0) == iota((n, n), 1), ids, 0), axis=1, keepdims=True)
    time_ids = iota((n, lanes), 1) % times + first_time
    angles = angles_of(column, time_ids)
    weights = jnp.exp2(time_ids.astype(jnp.float32) * (math.log2(DAMPING) / STEPS))
    table = jnp.concatenate([weights * jnp.cos(angles), -weights * jnp.sin(angles)], axis=0)
    row = iota((rows, 2 * n), 0)
    spread = (iota((rows, 2 * n), 1) == (row // CHUNKS) % 2 * n + row // (2 * CHUNKS)).astype(jnp.bfloat16)
    kept = iota((rows, lanes), 0) % CHUNKS == iota((rows, lanes), 1) // times
    hi, lo = [
        jnp.where(kept, jnp.dot(spread, part, preferred_element_type=jnp.float32), 0.0).astype(jnp.bfloat16)
        for part in split_f32(table)]
    return hi, lo


def inverse_matrix(ids, first_time, times):
    n = ids.shape[1]
    rows, lanes = CHUNKS * times, n * 2 * CHUNKS
    time_ids = iota((rows, n), 0) % times + first_time
    angles = angles_of(ids, time_ids)
    scales = jnp.exp2(time_ids.astype(jnp.float32) * (-math.log2(DAMPING) / STEPS)) / STEPS
    factor = scales * jnp.where((ids == 0) | (ids == STEPS // 2), 1.0, 2.0)
    table = jnp.concatenate([factor * jnp.cos(angles), -factor * jnp.sin(angles)], axis=1)
    lane = iota((2 * n, lanes), 1)
    spread = (iota((2 * n, lanes), 0) == (lane // CHUNKS) % 2 * n + lane // (2 * CHUNKS)).astype(jnp.bfloat16)
    kept = iota((rows, lanes), 1) % CHUNKS == iota((rows, lanes), 0) // times
    return [
        jnp.where(kept, jnp.dot(part, spread, preferred_element_type=jnp.float32), 0.0).astype(jnp.bfloat16)
        for part in split_f32(table)]


def place(zs, ys):
    me = lax.axis_index("freq")
    core = lax.rem(me, 2)
    y = lax.rem(me // 2, ys)
    z = me // (2 * ys)
    return z, y, core


def index_of(z, y, core, ys):
    return (z * ys + y) * 2 + core


def greet(targets):
    barrier = pltpu.get_barrier_semaphore()
    for target in targets:
        pl.semaphore_signal(barrier, inc=1, device_id={"freq": target}, device_id_type=MESH)
    return lambda: pl.semaphore_wait(barrier, len(targets))


def partners(z, y, core, zs, ys):
    targets = [index_of(z, y, 1 - core, ys)]
    targets += [index_of(z, lax.rem(y + s, ys), core, ys) for s in range(1, ys)]
    targets += [index_of(lax.rem(z + s, zs), y, core, ys) for s in range(1, zs)]
    return targets


def scatter_kernel(zs, ys, ids_ref, slip_ref, out_ref, acc, send0, recv0, send1, recv1, send2, recv2, *sems):
    ss0, rs0, ss1, rs1, ss2, rs2 = sems
    z, y, core = place(zs, ys)
    ready = greet(partners(z, y, core, zs, ys))
    times, width = slip_ref.shape[1], slip_ref.shape[2] // CHUNKS
    order = list(range(zs // 2, zs // 2 - zs, -1))
    order = [s % zs for s in order if s % zs] + [0]
    table_hi, table_lo = forward_matrix(ids_ref[...], index_of(z, y, core, ys) * times, times)
    table = jnp.concatenate([table_hi, table_hi, table_lo], axis=1)
    for j in range(3):
        x = jnp.concatenate([slip_ref[j, :, c * width:(c + 1) * width] for c in range(CHUNKS)], axis=0)
        hi, lo = split_f32(x)
        stack = jnp.concatenate([hi, lo, hi], axis=0)
        res = jnp.dot(table, stack, preferred_element_type=jnp.float32)
        res = res.reshape(zs * ys, 2, 2 * CHUNKS, width)
        first, second = res[:, 0], res[:, 1]
        own = jnp.where(core == 0, first, second)
        other = jnp.where(core == 0, second, first)
        acc[:, j] = own
        send0[:, j] = other.astype(jnp.bfloat16)
    ready()
    stage0 = {}
    for s in order:
        at = lax.rem(z + s, zs)
        rows = pl.ds(at * ys, ys)
        stage0[s] = pltpu.make_async_remote_copy(
            src_ref=send0.at[rows], dst_ref=recv0.at[rows], send_sem=ss0.at[s], recv_sem=rs0.at[s],
            device_id={"freq": index_of(z, y, 1 - core, ys)}, device_id_type=MESH)
        stage0[s].start()
    stage1, stage2 = {}, {}
    for s in order:
        at = lax.rem(z + s, zs)
        stage0[s].wait_recv()
        for step in range(1, ys):
            there = lax.rem(y + step, ys)
            block = at * ys + there
            send1[step - 1, at] = (acc[block] + recv0[block].astype(jnp.float32)).astype(jnp.bfloat16)
            stage1[s, step] = pltpu.make_async_remote_copy(
                src_ref=send1.at[step - 1, at], dst_ref=recv1.at[step - 1, at],
                send_sem=ss1.at[step - 1, s], recv_sem=rs1.at[step - 1, s],
                device_id={"freq": index_of(z, there, core, ys)}, device_id_type=MESH)
            stage1[s, step].start()
    for s in order:
        at = lax.rem(z + s, zs)
        block = at * ys + y
        total = acc[block] + recv0[block].astype(jnp.float32)
        for step in range(1, ys):
            stage1[s, step].wait_recv()
            total += recv1[step - 1, at].astype(jnp.float32)
        if s:
            send2[s - 1] = total.astype(jnp.bfloat16)
            stage2[s] = pltpu.make_async_remote_copy(
                src_ref=send2.at[s - 1], dst_ref=recv2.at[s - 1], send_sem=ss2.at[s - 1], recv_sem=rs2.at[s - 1],
                device_id={"freq": index_of(at, y, core, ys)}, device_id_type=MESH)
            stage2[s].start()
    for s in order[:-1]:
        stage2[s].wait_recv()
        total += recv2[s - 1].astype(jnp.float32)
    out_ref[...] = total
    for copies in (stage0, stage1, stage2):
        for copy in copies.values():
            copy.wait_send()


def scatter_spectra(ids, slip, zs, ys):
    block = (3, 2 * CHUNKS, slip.shape[2] // CHUNKS)
    bf16 = jnp.bfloat16
    high, many = max(ys - 1, 1), max(zs - 1, 1)
    return pl.pallas_call(
        functools.partial(scatter_kernel, zs, ys),
        out_shape=jax.ShapeDtypeStruct(block, jnp.float32),
        in_specs=[pl.BlockSpec(memory_space=pltpu.VMEM)] * 2,
        out_specs=pl.BlockSpec(memory_space=pltpu.VMEM),
        scratch_shapes=[
            pltpu.VMEM((zs * ys,) + block, jnp.float32),
            pltpu.VMEM((zs * ys,) + block, bf16),
            pltpu.VMEM((zs * ys,) + block, bf16),
            pltpu.VMEM((high, zs) + block, bf16),
            pltpu.VMEM((high, zs) + block, bf16),
            pltpu.VMEM((many,) + block, bf16),
            pltpu.VMEM((many,) + block, bf16),
            pltpu.SemaphoreType.DMA((zs,)),
            pltpu.SemaphoreType.DMA((zs,)),
            pltpu.SemaphoreType.DMA((high, zs)),
            pltpu.SemaphoreType.DMA((high, zs)),
            pltpu.SemaphoreType.DMA((many,)),
            pltpu.SemaphoreType.DMA((many,)),
        ],
        compiler_params=pltpu.CompilerParams(collective_id=0, has_side_effects=True, vmem_limit_bytes=(12 + zs * ys * 5 // 4) * MIB),
        name="spectra_scatter",
    )(ids, slip)


def operator_kernel(spec_ref, right_ref, coupling_ref, left_ref, rank_ref, col_ref, image_ref, coef, tiled, sums):
    f32, bf16 = jnp.float32, jnp.bfloat16
    groups = spec_ref.shape[2] // LEAF
    rank = right_ref.shape[3]
    clusters = groups * CHUNKS
    blocks = coupling_ref.shape[1]
    chunk_row = lax.broadcasted_iota(jnp.int32, (2 * CHUNKS, 2 * rank), 0) % CHUNKS
    half = CHUNKS // 2
    for g in range(groups):
        lanes = slice(g * LEAF, (g + 1) * LEAF)
        x = jnp.concatenate([spec_ref[j, :, lanes] for j in range(3)], axis=1)
        x = jnp.concatenate(split_f32(x), axis=0)
        prod = jnp.zeros((2 * CHUNKS, 2 * rank), f32)
        for h in range(2):
            basis = jnp.concatenate(
                [jnp.concatenate([right_ref[(h * half + c) * groups + g, q, j] for c in range(half) for q in range(2)], axis=0)
                 for j in range(3)], axis=1)
            full = lax.dot_general(x, basis, (((1,), (1,)), ((), ())), preferred_element_type=f32)
            full = full[:2 * CHUNKS] + full[2 * CHUNKS:]
            for c in range(half):
                prod = jnp.where(chunk_row == h * half + c, full[:, c * 2 * rank:(c + 1) * 2 * rank], prod)
        low, high = prod[:CHUNKS], prod[CHUNKS:]
        rows = slice(g * CHUNKS, (g + 1) * CHUNKS)
        coef[0, rows] = low[:, :rank] - high[:, rank:]
        coef[1, rows] = high[:, :rank] + low[:, rank:]
    square = (clusters, clusters)
    cluster_of = iota(square, 0) % CHUNKS * groups + iota(square, 0) // CHUNKS
    ranks = jnp.sum(jnp.where(iota(square, 1) == cluster_of, rank_ref[...], 0), axis=1, keepdims=True)
    kept = iota((clusters, rank), 1) < ranks
    area = rank * rank
    lane_of = lax.broadcasted_iota(jnp.int32, (rank, area), 1)
    spread = (lane_of % rank == lax.broadcasted_iota(jnp.int32, (rank, area), 0)).astype(bf16)
    for p in range(2):
        hi, lo = split_f32(jnp.where(kept, coef[p], 0.0))
        tiled[p] = jnp.dot(hi, spread, preferred_element_type=f32) + jnp.dot(lo, spread, preferred_element_type=f32)

    def couple(step, carry):
        found = [[], []]
        for r in range(4):
            a = step * 4 + r
            totals = [jnp.zeros((2, area), f32), jnp.zeros((2, area), f32)]
            for i in range(blocks):
                source = col_ref[i, a]
                row = (source % groups) * CHUNKS + source // groups
                block = coupling_ref[a, i].astype(f32)
                for p in range(2):
                    totals[p] = totals[p] + block * tiled[p, pl.ds(row, 1), :]
            found[0].append(totals[0])
            found[1].append(totals[1])
        for p in range(2):
            sums[p, pl.ds(pl.multiple_of(step * 8, 8), 8), :] = jnp.concatenate(found[p], axis=0)
        return carry

    lax.fori_loop(0, clusters // 4, couple, 0)
    row_of = lax.broadcasted_iota(jnp.int32, (area, rank), 0)
    gather = (row_of // rank == lax.broadcasted_iota(jnp.int32, (area, rank), 1)).astype(bf16)
    target = lax.broadcasted_iota(jnp.int32, (clusters, 2 * clusters), 0)
    origin = lax.broadcasted_iota(jnp.int32, (clusters, 2 * clusters), 1)
    cluster = (target % CHUNKS) * groups + target // CHUNKS
    picks = [(origin == 2 * cluster + q).astype(f32) for q in range(2)]
    parts = {}
    for p in range(2):
        hi, lo = split_f32(sums[p])
        short = jnp.dot(hi, gather, preferred_element_type=f32) + jnp.dot(lo, gather, preferred_element_type=f32)
        for q in range(2):
            parts[p, q] = jnp.dot(picks[q], short, precision=lax.Precision.HIGHEST, preferred_element_type=f32)
    real = jnp.where(kept, parts[0, 0] - parts[1, 1], 0.0)
    imag = jnp.where(kept, parts[1, 0] + parts[0, 1], 0.0)
    for g in range(groups):
        rows = slice(g * CHUNKS, (g + 1) * CHUNKS)
        mixed = jnp.concatenate([
            jnp.concatenate([real[rows], -imag[rows]], axis=1),
            jnp.concatenate([imag[rows], real[rows]], axis=1)], axis=0)
        masked = jnp.concatenate([jnp.where(chunk_row == c, mixed, 0.0) for c in range(CHUNKS)], axis=1)
        masked = jnp.concatenate(split_f32(masked), axis=0)
        for j in range(3):
            basis = jnp.concatenate([left_ref[c * groups + g, q, j] for c in range(CHUNKS) for q in range(2)], axis=0)
            out = jnp.dot(masked, basis, preferred_element_type=f32)
            out = out[:2 * CHUNKS] + out[2 * CHUNKS:]
            image_ref[j, :, g * LEAF:(g + 1) * LEAF] = out.astype(bf16)


def apply_operator(spectrum, right, coupling, left, ranks, col_clusters):
    clusters, rank = right.shape[0], right.shape[3]
    vmem = pl.BlockSpec(memory_space=pltpu.VMEM)
    return pl.pallas_call(
        operator_kernel,
        out_shape=jax.ShapeDtypeStruct(spectrum.shape, jnp.bfloat16),
        in_specs=[vmem] * 5 + [pl.BlockSpec(memory_space=pltpu.SMEM)],
        out_specs=vmem,
        scratch_shapes=[
            pltpu.VMEM((2, clusters, rank), jnp.float32),
            pltpu.VMEM((2, clusters, rank * rank), jnp.float32),
            pltpu.VMEM((2, 2 * clusters, rank * rank), jnp.float32),
        ],
        compiler_params=pltpu.CompilerParams(vmem_limit_bytes=24 * MIB),
        name="operator",
    )(spectrum, right, coupling, left, ranks, col_clusters.T)


def gather_kernel(zs, ys, times, image_ref, ids_ref, out_ref, hi_ref, lo_ref, local_sem, *sems):
    zsend, zrecv, ysend, yrecv, csend, crecv = sems
    z, y, core = place(zs, ys)
    ready = greet(partners(z, y, core, zs, ys))
    me = index_of(z, y, core, ys)
    mine = pltpu.make_async_copy(image_ref, out_ref.at[me], local_sem)
    mine.start()
    ready()
    copies = []

    def send(block, j, source, target, send_sem, recv_sem):
        copy = pltpu.make_async_remote_copy(
            src_ref=source.at[j], dst_ref=out_ref.at[block, j], send_sem=send_sem, recv_sem=recv_sem,
            device_id={"freq": target}, device_id_type=MESH)
        copy.start()
        copies.append(copy)

    other = index_of(z, y, 1 - core, ys)
    far = sorted(range(1, zs), key=lambda s: -min(s, zs - s))
    near = far[::-1]

    def pass_y(block, j, source, s):
        for step in range(1, ys):
            send(block, j, source, index_of(z, lax.rem(y + step, ys), core, ys),
                 ysend.at[step - 1, s, j], yrecv.at[step - 1, s, j])

    def arrived(block, j, recv_sem):
        pltpu.make_async_copy(out_ref.at[block, j], out_ref.at[block, j], recv_sem).wait()

    pieces = range(3)
    for j in pieces:
        for s in far:
            send(me, j, image_ref, index_of(lax.rem(z + s, zs), y, core, ys), zsend.at[s - 1, j], zrecv.at[s - 1, j])
        pass_y(me, j, image_ref, 0)
        send(me, j, image_ref, other, csend.at[0, 0, j], crecv.at[0, 0, j])
    hi_ref[...], lo_ref[...] = inverse_matrix(ids_ref[...], me * times, times)

    for j in pieces:
        for s in near:
            block = index_of(lax.rem(z + zs - s, zs), y, core, ys)
            arrived(block, j, zrecv.at[s - 1, j])
            pass_y(block, j, out_ref.at[block], s)
            send(block, j, out_ref.at[block], other, csend.at[0, s, j], crecv.at[0, s, j])
    for j in pieces:
        for s in [0] + near:
            for step in range(1, ys):
                block = index_of(lax.rem(z + zs - s, zs), lax.rem(y + ys - step, ys), core, ys)
                arrived(block, j, yrecv.at[step - 1, s, j])
                send(block, j, out_ref.at[block], other, csend.at[step, s, j], crecv.at[step, s, j])
    for j in pieces:
        for s in [0] + near:
            for step in range(ys):
                block = index_of(lax.rem(z + zs - s, zs), lax.rem(y + ys - step, ys), 1 - core, ys)
                arrived(block, j, crecv.at[step, s, j])
    mine.wait()
    for copy in copies:
        copy.wait_send()


def gather_images(image, ids, times, zs, ys):
    high, many = max(ys - 1, 1), max(zs - 1, 1)
    n = zs * ys * 2
    vmem = pl.BlockSpec(memory_space=pltpu.VMEM)
    matrix = jax.ShapeDtypeStruct((CHUNKS * times, n * 2 * CHUNKS), jnp.bfloat16)
    return pl.pallas_call(
        functools.partial(gather_kernel, zs, ys, times),
        out_shape=(jax.ShapeDtypeStruct((n,) + image.shape, image.dtype), matrix, matrix),
        in_specs=[vmem, vmem],
        out_specs=(vmem, vmem, vmem),
        scratch_shapes=[
            pltpu.SemaphoreType.DMA,
            pltpu.SemaphoreType.DMA((many, 3)),
            pltpu.SemaphoreType.DMA((many, 3)),
            pltpu.SemaphoreType.DMA((high, zs, 3)),
            pltpu.SemaphoreType.DMA((high, zs, 3)),
            pltpu.SemaphoreType.DMA((ys, zs, 3)),
            pltpu.SemaphoreType.DMA((ys, zs, 3)),
        ],
        compiler_params=pltpu.CompilerParams(collective_id=1, has_side_effects=True, vmem_limit_bytes=24 * MIB),
        name="image_gather",
    )(image, ids)


def synthesis_kernel(hi_ref, lo_ref, image_ref, out_ref):
    width, times = image_ref.shape[2], out_ref.shape[1]
    x = image_ref[...].reshape(-1, width)
    res = jnp.dot(hi_ref[...], x, preferred_element_type=jnp.float32)
    res += jnp.dot(lo_ref[...], x, preferred_element_type=jnp.float32)
    for c in range(CHUNKS):
        out_ref[0, :, c * width:(c + 1) * width] = res[c * times:(c + 1) * times]


def synthesize(hi, lo, images, times):
    n, _, rows, width = images.shape
    whole = pl.BlockSpec(hi.shape, lambda j: (0, 0))
    return pl.pallas_call(
        synthesis_kernel,
        grid=(3,),
        out_shape=jax.ShapeDtypeStruct((3, times, CHUNKS * width), jnp.float32),
        in_specs=[whole, whole, pl.BlockSpec((n, None, rows, width), lambda j: (0, j, 0, 0))],
        out_specs=pl.BlockSpec((1, times, CHUNKS * width), lambda j: (j, 0, 0)),
        compiler_params=pltpu.CompilerParams(vmem_limit_bytes=32 * MIB),
        name="synthesis",
    )(hi, lo, images)


def body(zs, ys, slip_history, frequency_ids, col_clusters, basis_ranks, left_basis, right_basis, coupling):
    times = slip_history.shape[0]
    ids = frequency_ids.reshape(1, -1)
    slip = jnp.transpose(slip_history, (1, 0, 2))
    right = jnp.transpose(right_basis[0], (0, 1, 3, 2, 4))
    left = jnp.transpose(left_basis[0], (0, 1, 3, 2, 4))
    spectrum = scatter_spectra(ids, slip, zs, ys)
    image = apply_operator(spectrum, right, coupling[0], left, basis_ranks, col_clusters)
    images, hi, lo = gather_images(image, ids, times, zs, ys)
    traction = synthesize(hi, lo, images, times)
    return jnp.transpose(traction, (1, 0, 2))


def solution(mesh):
    ys = max(4 // mesh.shape["group"], 1)
    zs = mesh.shape["freq"] // (2 * ys)
    return jax.shard_map(
        functools.partial(body, zs, ys),
        mesh=mesh,
        in_specs=(
            P("freq", None, "group"),
            P(),
            P(),
            P("freq", "group"),
            P("freq", "group", None, None, None, None),
            P("freq", "group", None, None, None, None),
            P("freq", "group", None, None, None),
        ),
        out_specs=P("freq", None, "group"),
        check_vma=False,
    )
```

```python
import functools
import math

import jax
import jax.numpy as jnp
from jax import lax
from jax.experimental import pallas as pl
from jax.experimental.pallas import tpu as pltpu
from jax.sharding import PartitionSpec as P

STEPS = 512
DAMPING = 0.5
LEAF = 128
CHUNKS = 8
MESH = pl.DeviceIdType.MESH
MIB = 1024 * 1024


def split_f32(x):
    hi = x.astype(jnp.bfloat16)
    lo = (x - hi.astype(jnp.float32)).astype(jnp.bfloat16)
    return hi, lo


def iota(shape, axis):
    return lax.broadcasted_iota(jnp.int32, shape, axis)


def angles_of(frequencies, times):
    phases = (frequencies * times) & (STEPS - 1)
    return phases.astype(jnp.float32) * (2.0 * math.pi / STEPS)


def forward_matrix(ids, first_time, times):
    n = ids.shape[1]
    lanes, rows = CHUNKS * times, n * 2 * CHUNKS
    column = jnp.sum(jnp.where(iota((n, n), 0) == iota((n, n), 1), ids, 0), axis=1, keepdims=True)
    time_ids = iota((n, lanes), 1) % times + first_time
    angles = angles_of(column, time_ids)
    weights = jnp.exp2(time_ids.astype(jnp.float32) * (math.log2(DAMPING) / STEPS))
    table = jnp.concatenate([weights * jnp.cos(angles), -weights * jnp.sin(angles)], axis=0)
    row = iota((rows, 2 * n), 0)
    spread = (iota((rows, 2 * n), 1) == (row // CHUNKS) % 2 * n + row // (2 * CHUNKS)).astype(jnp.bfloat16)
    kept = iota((rows, lanes), 0) % CHUNKS == iota((rows, lanes), 1) // times
    hi, lo = [
        jnp.where(kept, jnp.dot(spread, part, preferred_element_type=jnp.float32), 0.0).astype(jnp.bfloat16)
        for part in split_f32(table)]
    return hi, lo


def inverse_matrix(ids, first_time, times):
    n = ids.shape[1]
    rows, lanes = CHUNKS * times, n * 2 * CHUNKS
    time_ids = iota((rows, n), 0) % times + first_time
    angles = angles_of(ids, time_ids)
    scales = jnp.exp2(time_ids.astype(jnp.float32) * (-math.log2(DAMPING) / STEPS)) / STEPS
    factor = scales * jnp.where((ids == 0) | (ids == STEPS // 2), 1.0, 2.0)
    table = jnp.concatenate([factor * jnp.cos(angles), -factor * jnp.sin(angles)], axis=1)
    lane = iota((2 * n, lanes), 1)
    spread = (iota((2 * n, lanes), 0) == (lane // CHUNKS) % 2 * n + lane // (2 * CHUNKS)).astype(jnp.bfloat16)
    kept = iota((rows, lanes), 1) % CHUNKS == iota((rows, lanes), 0) // times
    return [
        jnp.where(kept, jnp.dot(part, spread, preferred_element_type=jnp.float32), 0.0).astype(jnp.bfloat16)
        for part in split_f32(table)]


def place(zs, ys):
    me = lax.axis_index("freq")
    core = lax.rem(me, 2)
    y = lax.rem(me // 2, ys)
    z = me // (2 * ys)
    return z, y, core


def index_of(z, y, core, ys):
    return (z * ys + y) * 2 + core


def greet(targets):
    barrier = pltpu.get_barrier_semaphore()
    for target in targets:
        pl.semaphore_signal(barrier, inc=1, device_id={"freq": target}, device_id_type=MESH)
    return lambda: pl.semaphore_wait(barrier, len(targets))


def partners(z, y, core, zs, ys):
    targets = [index_of(z, y, 1 - core, ys)]
    targets += [index_of(z, lax.rem(y + s, ys), core, ys) for s in range(1, ys)]
    targets += [index_of(lax.rem(z + s, zs), y, core, ys) for s in range(1, zs)]
    return targets


def scatter_phase(zs, ys, ready, ids, slip_ref, slip_sems, between, acc, send0, recv0, send1, recv1, send2, recv2, sems):
    ss0, rs0, ss1, rs1, ss2, rs2 = sems
    z, y, core = place(zs, ys)
    times, width = slip_ref.shape[1], slip_ref.shape[2] // CHUNKS
    order = list(range(zs // 2, zs // 2 - zs, -1))
    order = [s % zs for s in order if s % zs] + [0]
    table_hi, table_lo = forward_matrix(ids, index_of(z, y, core, ys) * times, times)
    table = jnp.concatenate([table_hi, table_hi, table_lo], axis=1)
    for j in range(3):
        pltpu.make_async_copy(slip_ref.at[j], slip_ref.at[j], slip_sems.at[j]).wait()
        x = jnp.concatenate([slip_ref[j, :, c * width:(c + 1) * width] for c in range(CHUNKS)], axis=0)
        hi, lo = split_f32(x)
        stack = jnp.concatenate([hi, lo, hi], axis=0)
        res = jnp.dot(table, stack, preferred_element_type=jnp.float32)
        res = res.reshape(zs * ys, 2, 2 * CHUNKS, width)
        first, second = res[:, 0], res[:, 1]
        own = jnp.where(core == 0, first, second)
        other = jnp.where(core == 0, second, first)
        acc[:, j] = own
        send0[:, j] = other.astype(jnp.bfloat16)
    ready()
    stage0 = {}
    for s in order:
        at = lax.rem(z + s, zs)
        rows = pl.ds(at * ys, ys)
        stage0[s] = pltpu.make_async_remote_copy(
            src_ref=send0.at[rows], dst_ref=recv0.at[rows], send_sem=ss0.at[s], recv_sem=rs0.at[s],
            device_id={"freq": index_of(z, y, 1 - core, ys)}, device_id_type=MESH)
        stage0[s].start()
    stage1, stage2 = {}, {}
    for s in order:
        at = lax.rem(z + s, zs)
        stage0[s].wait_recv()
        for step in range(1, ys):
            there = lax.rem(y + step, ys)
            block = at * ys + there
            send1[step - 1, at] = (acc[block] + recv0[block].astype(jnp.float32)).astype(jnp.bfloat16)
            stage1[s, step] = pltpu.make_async_remote_copy(
                src_ref=send1.at[step - 1, at], dst_ref=recv1.at[step - 1, at],
                send_sem=ss1.at[step - 1, s], recv_sem=rs1.at[step - 1, s],
                device_id={"freq": index_of(z, there, core, ys)}, device_id_type=MESH)
            stage1[s, step].start()
    between()
    for s in order:
        at = lax.rem(z + s, zs)
        block = at * ys + y
        total = acc[block] + recv0[block].astype(jnp.float32)
        for step in range(1, ys):
            stage1[s, step].wait_recv()
            total += recv1[step - 1, at].astype(jnp.float32)
        if s:
            send2[s - 1] = total.astype(jnp.bfloat16)
            stage2[s] = pltpu.make_async_remote_copy(
                src_ref=send2.at[s - 1], dst_ref=recv2.at[s - 1], send_sem=ss2.at[s - 1], recv_sem=rs2.at[s - 1],
                device_id={"freq": index_of(at, y, core, ys)}, device_id_type=MESH)
            stage2[s].start()
    for s in order[:-1]:
        stage2[s].wait_recv()
        total += recv2[s - 1].astype(jnp.float32)
    for copies in (stage0, stage1, stage2):
        for copy in copies.values():
            copy.wait_send()
    return total


def reorder_coupling(coupling_ref, ordered):
    groups, blocks = coupling_ref.shape[0] // CHUNKS, coupling_ref.shape[1]

    def step(g, carry):
        rows = pl.ds(pl.multiple_of(g * CHUNKS, CHUNKS), CHUNKS)
        for i in range(blocks):
            found = [coupling_ref[c * groups + g, i].astype(jnp.float32) for c in range(CHUNKS)]
            for q in range(2):
                ordered[q, i, rows, :] = jnp.concatenate([part[q:q + 1] for part in found], axis=0)
        return carry

    lax.fori_loop(0, groups, step, 0)


def operator_phase(spectrum, right_ref, ordered, left_ref, wait_left, rank_row, col_ref, image_ref, coef):
    f32, bf16 = jnp.float32, jnp.bfloat16
    groups = spectrum.shape[2] // LEAF
    rank = right_ref.shape[3]
    clusters = groups * CHUNKS
    blocks = ordered.shape[1]
    chunk_row = lax.broadcasted_iota(jnp.int32, (2 * CHUNKS, 2 * rank), 0) % CHUNKS
    half = CHUNKS // 2
    for g in range(groups):
        lanes = slice(g * LEAF, (g + 1) * LEAF)
        x = jnp.concatenate([spectrum[j, :, lanes] for j in range(3)], axis=1)
        x = jnp.concatenate(split_f32(x), axis=0)
        prod = jnp.zeros((2 * CHUNKS, 2 * rank), f32)
        for h in range(2):
            basis = jnp.concatenate(
                [jnp.concatenate([right_ref[(h * half + c) * groups + g, q, j] for c in range(half) for q in range(2)], axis=0)
                 for j in range(3)], axis=1)
            full = lax.dot_general(x, basis, (((1,), (1,)), ((), ())), preferred_element_type=f32)
            full = full[:2 * CHUNKS] + full[2 * CHUNKS:]
            for c in range(half):
                prod = jnp.where(chunk_row == h * half + c, full[:, c * 2 * rank:(c + 1) * 2 * rank], prod)
        low, high = prod[:CHUNKS], prod[CHUNKS:]
        rows = slice(g * CHUNKS, (g + 1) * CHUNKS)
        coef[0, rows] = low[:, :rank] - high[:, rank:]
        coef[1, rows] = high[:, :rank] + low[:, rank:]
    square = (clusters, clusters)
    cluster_of = iota(square, 0) % CHUNKS * groups + iota(square, 0) // CHUNKS
    ranks = jnp.sum(jnp.where(iota(square, 1) == cluster_of, rank_row, 0), axis=1, keepdims=True)
    kept = iota((clusters, rank), 1) < ranks
    area = rank * rank
    spread = (iota((2 * rank, area), 1) % rank == iota((2 * rank, area), 0) % rank).astype(bf16)
    held = [jnp.concatenate(split_f32(jnp.where(kept, coef[p], 0.0)), axis=1) for p in range(2)]
    sums = [jnp.zeros((clusters, area), f32) for _ in range(2)]
    for i in range(blocks):
        sources = jnp.sum(jnp.where(iota(square, 1) == cluster_of, col_ref[i:i + 1, :], 0), axis=1, keepdims=True)
        source_rows = sources % groups * CHUNKS + sources // groups
        pick = (iota(square, 1) == source_rows).astype(bf16)
        real, imag = [
            jnp.dot(jnp.dot(pick, part, preferred_element_type=f32).astype(bf16), spread, preferred_element_type=f32)
            for part in held]
        low, high = ordered[0, i], ordered[1, i]
        sums[0] += low * real - high * imag
        sums[1] += high * real + low * imag
    gather = (iota((area, rank), 0) // rank == iota((area, rank), 1)).astype(bf16)
    middle = []
    for part in sums:
        hi, lo = split_f32(part)
        short = jnp.dot(hi, gather, preferred_element_type=f32) + jnp.dot(lo, gather, preferred_element_type=f32)
        middle.append(jnp.where(kept, short, 0.0))
    real, imag = middle
    wait_left()
    for g in range(groups):
        rows = slice(g * CHUNKS, (g + 1) * CHUNKS)
        mixed = jnp.concatenate([
            jnp.concatenate([real[rows], -imag[rows]], axis=1),
            jnp.concatenate([imag[rows], real[rows]], axis=1)], axis=0)
        masked = jnp.concatenate([jnp.where(chunk_row == c, mixed, 0.0) for c in range(CHUNKS)], axis=1)
        masked = jnp.concatenate(split_f32(masked), axis=0)
        for j in range(3):
            basis = jnp.concatenate([left_ref[c * groups + g, q, j] for c in range(CHUNKS) for q in range(2)], axis=0)
            out = jnp.dot(masked, basis, preferred_element_type=f32)
            out = out[:2 * CHUNKS] + out[2 * CHUNKS:]
            image_ref[j, :, g * LEAF:(g + 1) * LEAF] = out.astype(bf16)


def gather_phase(zs, ys, image_ref, out_ref, local_sem, meanwhile, finish, sems):
    zsend, zrecv, ysend, yrecv, csend, crecv = sems
    z, y, core = place(zs, ys)
    me = index_of(z, y, core, ys)
    mine = pltpu.make_async_copy(image_ref, out_ref.at[me], local_sem)
    mine.start()
    copies = []

    def send(block, j, source, target, send_sem, recv_sem):
        copy = pltpu.make_async_remote_copy(
            src_ref=source.at[j], dst_ref=out_ref.at[block, j], send_sem=send_sem, recv_sem=recv_sem,
            device_id={"freq": target}, device_id_type=MESH)
        copy.start()
        copies.append(copy)

    other = index_of(z, y, 1 - core, ys)
    far = sorted(range(1, zs), key=lambda s: -min(s, zs - s))
    near = far[::-1]

    def pass_y(block, j, source, s):
        for step in range(1, ys):
            send(block, j, source, index_of(z, lax.rem(y + step, ys), core, ys),
                 ysend.at[step - 1, s, j], yrecv.at[step - 1, s, j])

    def arrived(block, j, recv_sem):
        pltpu.make_async_copy(out_ref.at[block, j], out_ref.at[block, j], recv_sem).wait()

    for j in range(3):
        for s in far:
            send(me, j, image_ref, index_of(lax.rem(z + s, zs), y, core, ys), zsend.at[s - 1, j], zrecv.at[s - 1, j])
        pass_y(me, j, image_ref, 0)
        send(me, j, image_ref, other, csend.at[0, 0, j], crecv.at[0, 0, j])
    meanwhile()

    def from_z(j):
        for s in near:
            block = index_of(lax.rem(z + zs - s, zs), y, core, ys)
            arrived(block, j, zrecv.at[s - 1, j])
            pass_y(block, j, out_ref.at[block], s)
            send(block, j, out_ref.at[block], other, csend.at[0, s, j], crecv.at[0, s, j])

    def from_y(j):
        for s in [0] + near:
            for step in range(1, ys):
                block = index_of(lax.rem(z + zs - s, zs), lax.rem(y + ys - step, ys), core, ys)
                arrived(block, j, yrecv.at[step - 1, s, j])
                send(block, j, out_ref.at[block], other, csend.at[step, s, j], crecv.at[step, s, j])

    def from_core(j):
        for s in [0] + near:
            for step in range(ys):
                block = index_of(lax.rem(z + zs - s, zs), lax.rem(y + ys - step, ys), 1 - core, ys)
                arrived(block, j, crecv.at[step, s, j])
        finish(j)

    from_z(0)
    from_z(1)
    from_y(0)
    from_z(2)
    from_y(1)
    mine.wait()
    from_core(0)
    from_y(2)
    from_core(1)
    from_core(2)
    for copy in copies:
        copy.wait_send()


def traction_kernel(zs, ys, *refs):
    ids_ref, rank_ref, col_ref, slip_hbm, right_hbm, coupling_hbm, left_hbm = refs[:7]
    traction_hbm, images, hi_ref, lo_ref = refs[7:11]
    slip, right, coupling, left, ordered, coef, image, fetch_sems, local_sem = refs[11:20]
    scatter_refs, scatter_sems, gather_sems = refs[20:27], refs[27:33], refs[33:]
    z, y, core = place(zs, ys)
    ready = greet(partners(z, y, core, zs, ys))
    for j in range(3):
        pltpu.make_async_copy(slip_hbm.at[j], slip.at[j], fetch_sems.at[j]).start()
    fetches = [
        pltpu.make_async_copy(source, target, fetch_sems.at[3 + at])
        for at, (source, target) in enumerate([(coupling_hbm, coupling), (right_hbm, right), (left_hbm, left)])]
    for fetch in fetches:
        fetch.start()

    def between():
        fetches[0].wait()
        reorder_coupling(coupling, ordered)

    spectrum = scatter_phase(zs, ys, ready, ids_ref[...], slip, fetch_sems, between, *scatter_refs, scatter_sems)
    fetches[1].wait()
    operator_phase(spectrum, right, ordered, left, fetches[2].wait, rank_ref[...], col_ref, image, coef)
    times = slip.shape[1]

    def meanwhile():
        hi_ref[...], lo_ref[...] = inverse_matrix(ids_ref[...], index_of(z, y, core, ys) * times, times)

    traction, width = slip, image.shape[2]
    stores = [pltpu.make_async_copy(traction.at[j], traction_hbm.at[j], fetch_sems.at[j]) for j in range(3)]

    def finish(j):
        x = images[:, j].reshape(-1, width)
        res = jnp.dot(hi_ref[...], x, preferred_element_type=jnp.float32)
        res += jnp.dot(lo_ref[...], x, preferred_element_type=jnp.float32)
        for c in range(CHUNKS):
            traction[j, :, c * width:(c + 1) * width] = res[c * times:(c + 1) * times]
        stores[j].start()

    gather_phase(zs, ys, image, images, local_sem, meanwhile, finish, gather_sems)
    for store in stores:
        store.wait()


def all_tractions(ids, ranks, cols, slip, right, coupling, left, zs, ys):
    times, n = slip.shape[1], zs * ys * 2
    clusters, rank, blocks = right.shape[0], right.shape[3], coupling.shape[1]
    block = (3, 2 * CHUNKS, slip.shape[2] // CHUNKS)
    f32, bf16 = jnp.float32, jnp.bfloat16
    high, many = max(ys - 1, 1), max(zs - 1, 1)
    middle = (high, zs) if ys > 1 else (1, 1)
    vmem, hbm = pl.BlockSpec(memory_space=pltpu.VMEM), pl.BlockSpec(memory_space=pl.ANY)
    matrix = pltpu.VMEM((CHUNKS * times, n * 2 * CHUNKS), bf16)
    dma = pltpu.SemaphoreType.DMA
    return pl.pallas_call(
        functools.partial(traction_kernel, zs, ys),
        out_shape=jax.ShapeDtypeStruct(slip.shape, f32),
        in_specs=[vmem, vmem, vmem, hbm, hbm, hbm, hbm],
        out_specs=hbm,
        scratch_shapes=[
            pltpu.VMEM((n,) + block, bf16),
            matrix,
            matrix,
            pltpu.VMEM(slip.shape, f32),
            pltpu.VMEM(right.shape, bf16),
            pltpu.VMEM(coupling.shape, bf16),
            pltpu.VMEM(left.shape, bf16),
            pltpu.VMEM((2, blocks, clusters, rank * rank), f32),
            pltpu.VMEM((2, clusters, rank), f32),
            pltpu.VMEM(block, bf16),
            dma((6,)),
            dma,
            pltpu.VMEM((zs * ys,) + block, f32),
            pltpu.VMEM((zs * ys,) + block, bf16),
            pltpu.VMEM((zs * ys,) + block, bf16),
            pltpu.VMEM(middle + block, bf16),
            pltpu.VMEM(middle + block, bf16),
            pltpu.VMEM((many,) + block, bf16),
            pltpu.VMEM((many,) + block, bf16),
            dma((zs,)), dma((zs,)), dma((high, zs)), dma((high, zs)), dma((many,)), dma((many,)),
            dma((many, 3)), dma((many, 3)), dma((high, zs, 3)), dma((high, zs, 3)), dma((ys, zs, 3)), dma((ys, zs, 3)),
        ],
        compiler_params=pltpu.CompilerParams(
            collective_id=0, has_side_effects=True, vmem_limit_bytes=60 * MIB),
        name="traction",
    )(ids, ranks, cols, slip, right, coupling, left)


def body(zs, ys, slip_history, frequency_ids, col_clusters, basis_ranks, left_basis, right_basis, coupling):
    ids = frequency_ids.reshape(1, -1)
    slip = jnp.transpose(slip_history, (1, 0, 2))
    right = jnp.transpose(right_basis[0], (0, 1, 3, 2, 4))
    left = jnp.transpose(left_basis[0], (0, 1, 3, 2, 4))
    traction = all_tractions(
        ids, basis_ranks, col_clusters.T, slip, right, coupling[0], left, zs, ys)
    return jnp.transpose(traction, (1, 0, 2))


def solution(mesh):
    ys = max(4 // mesh.shape["group"], 1)
    zs = mesh.shape["freq"] // (2 * ys)
    return jax.shard_map(
        functools.partial(body, zs, ys),
        mesh=mesh,
        in_specs=(
            P("freq", None, "group"),
            P(),
            P(),
            P("freq", "group"),
            P("freq", "group", None, None, None, None),
            P("freq", "group", None, None, None, None),
            P("freq", "group", None, None, None),
        ),
        out_specs=P("freq", None, "group"),
        check_vma=False,
    )
```

```python
import functools
import math

import jax
import jax.numpy as jnp
from jax import lax
from jax.experimental import pallas as pl
from jax.experimental.pallas import tpu as pltpu
from jax.sharding import PartitionSpec as P

STEPS = 512
DAMPING = 0.5
LEAF = 128
CHUNKS = 8
MESH = pl.DeviceIdType.MESH
MIB = 1024 * 1024


def split_f32(x):
    hi = x.astype(jnp.bfloat16)
    lo = (x - hi.astype(jnp.float32)).astype(jnp.bfloat16)
    return hi, lo


def iota(shape, axis):
    return lax.broadcasted_iota(jnp.int32, shape, axis)


def angles_of(frequencies, times):
    phases = (frequencies * times) & (STEPS - 1)
    return phases.astype(jnp.float32) * (2.0 * math.pi / STEPS)


def forward_matrix(ids, first_time, times):
    n = ids.shape[1]
    lanes, rows = CHUNKS * times, n * 2 * CHUNKS
    column = jnp.sum(jnp.where(iota((n, n), 0) == iota((n, n), 1), ids, 0), axis=1, keepdims=True)
    time_ids = iota((n, lanes), 1) % times + first_time
    angles = angles_of(column, time_ids)
    weights = jnp.exp2(time_ids.astype(jnp.float32) * (math.log2(DAMPING) / STEPS))
    table = jnp.concatenate([weights * jnp.cos(angles), -weights * jnp.sin(angles)], axis=0)
    row = iota((rows, 2 * n), 0)
    spread = (iota((rows, 2 * n), 1) == (row // CHUNKS) % 2 * n + row // (2 * CHUNKS)).astype(jnp.bfloat16)
    kept = iota((rows, lanes), 0) % CHUNKS == iota((rows, lanes), 1) // times
    hi, lo = [
        jnp.where(kept, jnp.dot(spread, part, preferred_element_type=jnp.float32), 0.0).astype(jnp.bfloat16)
        for part in split_f32(table)]
    return hi, lo


def inverse_matrix(ids, first_time, times):
    n = ids.shape[1]
    rows, lanes = CHUNKS * times, n * 2 * CHUNKS
    time_ids = iota((rows, n), 0) % times + first_time
    angles = angles_of(ids, time_ids)
    scales = jnp.exp2(time_ids.astype(jnp.float32) * (-math.log2(DAMPING) / STEPS)) / STEPS
    factor = scales * jnp.where((ids == 0) | (ids == STEPS // 2), 1.0, 2.0)
    table = jnp.concatenate([factor * jnp.cos(angles), -factor * jnp.sin(angles)], axis=1)
    lane = iota((2 * n, lanes), 1)
    spread = (iota((2 * n, lanes), 0) == (lane // CHUNKS) % 2 * n + lane // (2 * CHUNKS)).astype(jnp.bfloat16)
    kept = iota((rows, lanes), 1) % CHUNKS == iota((rows, lanes), 0) // times
    return [
        jnp.where(kept, jnp.dot(part, spread, preferred_element_type=jnp.float32), 0.0).astype(jnp.bfloat16)
        for part in split_f32(table)]


def place(zs, ys):
    me = lax.axis_index("freq")
    core = lax.rem(me, 2)
    y = lax.rem(me // 2, ys)
    z = me // (2 * ys)
    return z, y, core


def index_of(z, y, core, ys):
    return (z * ys + y) * 2 + core


def greet(targets):
    barrier = pltpu.get_barrier_semaphore()
    for target in targets:
        pl.semaphore_signal(barrier, inc=1, device_id={"freq": target}, device_id_type=MESH)
    return lambda: pl.semaphore_wait(barrier, len(targets))


def partners(z, y, core, zs, ys):
    targets = [index_of(z, y, 1 - core, ys)]
    targets += [index_of(z, lax.rem(y + s, ys), core, ys) for s in range(1, ys)]
    targets += [index_of(lax.rem(z + s, zs), y, core, ys) for s in range(1, zs)]
    return targets


def scatter_phase(zs, ys, ready, ids, slip_ref, slip_sems, between, acc, send0, recv0, send1, recv1, send2, recv2, sems):
    ss0, rs0, ss1, rs1, ss2, rs2 = sems
    z, y, core = place(zs, ys)
    times, width = slip_ref.shape[1], slip_ref.shape[2] // CHUNKS
    order = list(range(zs // 2, zs // 2 - zs, -1))
    order = [s % zs for s in order if s % zs] + [0]
    table_hi, table_lo = forward_matrix(ids, index_of(z, y, core, ys) * times, times)
    table = jnp.concatenate([table_hi, table_hi, table_lo], axis=1)
    stage0, stage1, stage2 = {}, {}, {}

    def transform(j):
        pltpu.make_async_copy(slip_ref.at[j], slip_ref.at[j], slip_sems.at[j]).wait()
        x = jnp.concatenate([slip_ref[j, :, c * width:(c + 1) * width] for c in range(CHUNKS)], axis=0)
        hi, lo = split_f32(x)
        stack = jnp.concatenate([hi, lo, hi], axis=0)
        res = jnp.dot(table, stack, preferred_element_type=jnp.float32)
        res = res.reshape(zs * ys, 2, 2 * CHUNKS, width)
        first, second = res[:, 0], res[:, 1]
        acc[:, j] = jnp.where(core == 0, first, second)
        send0[:, j] = jnp.where(core == 0, second, first).astype(jnp.bfloat16)
        if j == 0:
            ready()
        stage0[j] = pltpu.make_async_remote_copy(
            src_ref=send0.at[:, j], dst_ref=recv0.at[:, j], send_sem=ss0.at[j], recv_sem=rs0.at[j],
            device_id={"freq": index_of(z, y, 1 - core, ys)}, device_id_type=MESH)
        stage0[j].start()

    def to_y(j):
        stage0[j].wait_recv()
        for step in range(1, ys):
            there = lax.rem(y + step, ys)
            for at in range(zs):
                block = at * ys + there
                send1[step - 1, at, j] = (acc[block, j] + recv0[block, j].astype(jnp.float32)).astype(jnp.bfloat16)
            stage1[step, j] = pltpu.make_async_remote_copy(
                src_ref=send1.at[step - 1, :, j], dst_ref=recv1.at[step - 1, :, j],
                send_sem=ss1.at[step - 1, j], recv_sem=rs1.at[step - 1, j],
                device_id={"freq": index_of(z, there, core, ys)}, device_id_type=MESH)
            stage1[step, j].start()

    def to_z(j):
        for step in range(1, ys):
            stage1[step, j].wait_recv()
        for s in order:
            at = lax.rem(z + s, zs)
            block = at * ys + y
            total = acc[block, j] + recv0[block, j].astype(jnp.float32)
            for step in range(1, ys):
                total += recv1[step - 1, at, j].astype(jnp.float32)
            if s:
                send2[s - 1, j] = total.astype(jnp.bfloat16)
                stage2[s, j] = pltpu.make_async_remote_copy(
                    src_ref=send2.at[s - 1, j], dst_ref=recv2.at[s - 1, j],
                    send_sem=ss2.at[s - 1, j], recv_sem=rs2.at[s - 1, j],
                    device_id={"freq": index_of(at, y, core, ys)}, device_id_type=MESH)
                stage2[s, j].start()
        return total

    transform(0)
    transform(1)
    to_y(0)
    transform(2)
    to_y(1)
    between(0, 1)
    to_y(2)
    between(1, 3)
    totals = [to_z(0)]
    between(3, 5)
    totals.append(to_z(1))
    between(5, 7)
    totals.append(to_z(2))
    between(7, 8)
    for j in range(3):
        for s in order[:-1]:
            stage2[s, j].wait_recv()
            totals[j] += recv2[s - 1, j].astype(jnp.float32)
    total = jnp.stack(totals)
    for copies in (stage0, stage1, stage2):
        for copy in copies.values():
            copy.wait_send()
    return total


def reorder_coupling(coupling_ref, ordered, begin, end):
    groups, blocks = coupling_ref.shape[0] // CHUNKS, coupling_ref.shape[1]

    def step(g, carry):
        rows = pl.ds(pl.multiple_of(g * CHUNKS, CHUNKS), CHUNKS)
        for i in range(blocks):
            found = [coupling_ref[c * groups + g, i].astype(jnp.float32) for c in range(CHUNKS)]
            for q in range(2):
                ordered[q, i, rows, :] = jnp.concatenate([part[q:q + 1] for part in found], axis=0)
        return carry

    lax.fori_loop(begin, end, step, 0)


def operator_phase(spectrum, right_ref, ordered, left_ref, wait_left, rank_row, col_ref, image_ref, coef):
    f32, bf16 = jnp.float32, jnp.bfloat16
    groups = spectrum.shape[2] // LEAF
    rank = right_ref.shape[3]
    clusters = groups * CHUNKS
    blocks = ordered.shape[1]
    chunk_row = lax.broadcasted_iota(jnp.int32, (2 * CHUNKS, 2 * rank), 0) % CHUNKS
    half = CHUNKS // 2
    for g in range(groups):
        lanes = slice(g * LEAF, (g + 1) * LEAF)
        x = jnp.concatenate([spectrum[j, :, lanes] for j in range(3)], axis=1)
        x = jnp.concatenate(split_f32(x), axis=0)
        prod = jnp.zeros((2 * CHUNKS, 2 * rank), f32)
        for h in range(2):
            basis = jnp.concatenate(
                [jnp.concatenate([right_ref[(h * half + c) * groups + g, q, j] for c in range(half) for q in range(2)], axis=0)
                 for j in range(3)], axis=1)
            full = lax.dot_general(x, basis, (((1,), (1,)), ((), ())), preferred_element_type=f32)
            full = full[:2 * CHUNKS] + full[2 * CHUNKS:]
            for c in range(half):
                prod = jnp.where(chunk_row == h * half + c, full[:, c * 2 * rank:(c + 1) * 2 * rank], prod)
        low, high = prod[:CHUNKS], prod[CHUNKS:]
        rows = slice(g * CHUNKS, (g + 1) * CHUNKS)
        coef[0, rows] = low[:, :rank] - high[:, rank:]
        coef[1, rows] = high[:, :rank] + low[:, rank:]
    square = (clusters, clusters)
    cluster_of = iota(square, 0) % CHUNKS * groups + iota(square, 0) // CHUNKS
    ranks = jnp.sum(jnp.where(iota(square, 1) == cluster_of, rank_row, 0), axis=1, keepdims=True)
    kept = iota((clusters, rank), 1) < ranks
    area = rank * rank
    spread = (iota((2 * rank, area), 1) % rank == iota((2 * rank, area), 0) % rank).astype(bf16)
    held = [jnp.concatenate(split_f32(jnp.where(kept, coef[p], 0.0)), axis=1) for p in range(2)]
    sums = [jnp.zeros((clusters, area), f32) for _ in range(2)]
    for i in range(blocks):
        sources = jnp.sum(jnp.where(iota(square, 1) == cluster_of, col_ref[i:i + 1, :], 0), axis=1, keepdims=True)
        source_rows = sources % groups * CHUNKS + sources // groups
        pick = (iota(square, 1) == source_rows).astype(bf16)
        real, imag = [
            jnp.dot(jnp.dot(pick, part, preferred_element_type=f32).astype(bf16), spread, preferred_element_type=f32)
            for part in held]
        low, high = ordered[0, i], ordered[1, i]
        sums[0] += low * real - high * imag
        sums[1] += high * real + low * imag
    gather = (iota((area, rank), 0) // rank == iota((area, rank), 1)).astype(bf16)
    middle = []
    for part in sums:
        hi, lo = split_f32(part)
        short = jnp.dot(hi, gather, preferred_element_type=f32) + jnp.dot(lo, gather, preferred_element_type=f32)
        middle.append(jnp.where(kept, short, 0.0))
    real, imag = middle
    wait_left()
    for g in range(groups):
        rows = slice(g * CHUNKS, (g + 1) * CHUNKS)
        mixed = jnp.concatenate([
            jnp.concatenate([real[rows], -imag[rows]], axis=1),
            jnp.concatenate([imag[rows], real[rows]], axis=1)], axis=0)
        masked = jnp.concatenate([jnp.where(chunk_row == c, mixed, 0.0) for c in range(CHUNKS)], axis=1)
        masked = jnp.concatenate(split_f32(masked), axis=0)
        for j in range(3):
            basis = jnp.concatenate([left_ref[c * groups + g, q, j] for c in range(CHUNKS) for q in range(2)], axis=0)
            out = jnp.dot(masked, basis, preferred_element_type=f32)
            out = out[:2 * CHUNKS] + out[2 * CHUNKS:]
            image_ref[j, :, g * LEAF:(g + 1) * LEAF] = out.astype(bf16)


def gather_phase(zs, ys, image_ref, out_ref, local_sem, meanwhile, finish, sems):
    zsend, zrecv, ysend, yrecv, csend, crecv = sems
    z, y, core = place(zs, ys)
    me = index_of(z, y, core, ys)
    mine = pltpu.make_async_copy(image_ref, out_ref.at[me], local_sem)
    mine.start()
    copies = []

    def send(block, j, source, target, send_sem, recv_sem):
        copy = pltpu.make_async_remote_copy(
            src_ref=source.at[j], dst_ref=out_ref.at[block, j], send_sem=send_sem, recv_sem=recv_sem,
            device_id={"freq": target}, device_id_type=MESH)
        copy.start()
        copies.append(copy)

    other = index_of(z, y, 1 - core, ys)
    far = sorted(range(1, zs), key=lambda s: -min(s, zs - s))
    near = far[::-1]

    def pass_y(block, j, source, s):
        for step in range(1, ys):
            send(block, j, source, index_of(z, lax.rem(y + step, ys), core, ys),
                 ysend.at[step - 1, s, j], yrecv.at[step - 1, s, j])

    def arrived(block, j, recv_sem):
        pltpu.make_async_copy(out_ref.at[block, j], out_ref.at[block, j], recv_sem).wait()

    for j in range(3):
        for s in far:
            send(me, j, image_ref, index_of(lax.rem(z + s, zs), y, core, ys), zsend.at[s - 1, j], zrecv.at[s - 1, j])
        pass_y(me, j, image_ref, 0)
        send(me, j, image_ref, other, csend.at[0, 0, j], crecv.at[0, 0, j])
    meanwhile()

    def from_z(j):
        for s in near:
            block = index_of(lax.rem(z + zs - s, zs), y, core, ys)
            arrived(block, j, zrecv.at[s - 1, j])
            pass_y(block, j, out_ref.at[block], s)
            send(block, j, out_ref.at[block], other, csend.at[0, s, j], crecv.at[0, s, j])

    def from_y(j):
        for s in [0] + near:
            for step in range(1, ys):
                block = index_of(lax.rem(z + zs - s, zs), lax.rem(y + ys - step, ys), core, ys)
                arrived(block, j, yrecv.at[step - 1, s, j])
                send(block, j, out_ref.at[block], other, csend.at[step, s, j], crecv.at[step, s, j])

    def from_core(j):
        for s in [0] + near:
            for step in range(ys):
                block = index_of(lax.rem(z + zs - s, zs), lax.rem(y + ys - step, ys), 1 - core, ys)
                arrived(block, j, crecv.at[step, s, j])
        finish(j)

    from_z(0)
    from_z(1)
    from_y(0)
    from_z(2)
    from_y(1)
    mine.wait()
    from_core(0)
    from_y(2)
    from_core(1)
    from_core(2)
    for copy in copies:
        copy.wait_send()


def traction_kernel(zs, ys, *refs):
    ids_ref, rank_ref, col_ref, slip_hbm, right_hbm, coupling_hbm, left_hbm = refs[:7]
    traction_hbm, images, hi_ref, lo_ref = refs[7:11]
    slip, right, coupling, left, ordered, coef, image, fetch_sems, local_sem = refs[11:20]
    scatter_refs, scatter_sems, gather_sems = refs[20:27], refs[27:33], refs[33:]
    z, y, core = place(zs, ys)
    ready = greet(partners(z, y, core, zs, ys))
    for j in range(3):
        pltpu.make_async_copy(slip_hbm.at[j], slip.at[j], fetch_sems.at[j]).start()
    fetches = [
        pltpu.make_async_copy(source, target, fetch_sems.at[3 + at])
        for at, (source, target) in enumerate([(coupling_hbm, coupling), (right_hbm, right), (left_hbm, left)])]
    for fetch in fetches:
        fetch.start()

    def between(begin, end):
        if begin == 0:
            fetches[0].wait()
        groups = coupling.shape[0] // CHUNKS
        reorder_coupling(coupling, ordered, begin * groups // 8, end * groups // 8)

    spectrum = scatter_phase(zs, ys, ready, ids_ref[...], slip, fetch_sems, between, *scatter_refs, scatter_sems)
    fetches[1].wait()
    operator_phase(spectrum, right, ordered, left, fetches[2].wait, rank_ref[...], col_ref, image, coef)
    times = slip.shape[1]

    def meanwhile():
        hi_ref[...], lo_ref[...] = inverse_matrix(ids_ref[...], index_of(z, y, core, ys) * times, times)

    traction, width = slip, image.shape[2]
    stores = [pltpu.make_async_copy(traction.at[j], traction_hbm.at[j], fetch_sems.at[j]) for j in range(3)]

    def finish(j):
        x = images[:, j].reshape(-1, width)
        res = jnp.dot(hi_ref[...], x, preferred_element_type=jnp.float32)
        res += jnp.dot(lo_ref[...], x, preferred_element_type=jnp.float32)
        for c in range(CHUNKS):
            traction[j, :, c * width:(c + 1) * width] = res[c * times:(c + 1) * times]
        stores[j].start()

    gather_phase(zs, ys, image, images, local_sem, meanwhile, finish, gather_sems)
    for store in stores:
        store.wait()


def all_tractions(ids, ranks, cols, slip, right, coupling, left, zs, ys):
    times, n = slip.shape[1], zs * ys * 2
    clusters, rank, blocks = right.shape[0], right.shape[3], coupling.shape[1]
    block = (3, 2 * CHUNKS, slip.shape[2] // CHUNKS)
    f32, bf16 = jnp.float32, jnp.bfloat16
    high, many = max(ys - 1, 1), max(zs - 1, 1)
    middle = (high, zs) if ys > 1 else (1, 1)
    vmem, hbm = pl.BlockSpec(memory_space=pltpu.VMEM), pl.BlockSpec(memory_space=pl.ANY)
    matrix = pltpu.VMEM((CHUNKS * times, n * 2 * CHUNKS), bf16)
    dma = pltpu.SemaphoreType.DMA
    return pl.pallas_call(
        functools.partial(traction_kernel, zs, ys),
        out_shape=jax.ShapeDtypeStruct(slip.shape, f32),
        in_specs=[vmem, vmem, vmem, hbm, hbm, hbm, hbm],
        out_specs=hbm,
        scratch_shapes=[
            pltpu.VMEM((n,) + block, bf16),
            matrix,
            matrix,
            pltpu.VMEM(slip.shape, f32),
            pltpu.VMEM(right.shape, bf16),
            pltpu.VMEM(coupling.shape, bf16),
            pltpu.VMEM(left.shape, bf16),
            pltpu.VMEM((2, blocks, clusters, rank * rank), f32),
            pltpu.VMEM((2, clusters, rank), f32),
            pltpu.VMEM(block, bf16),
            dma((6,)),
            dma,
            pltpu.VMEM((zs * ys,) + block, f32),
            pltpu.VMEM((zs * ys,) + block, bf16),
            pltpu.VMEM((zs * ys,) + block, bf16),
            pltpu.VMEM(middle + block, bf16),
            pltpu.VMEM(middle + block, bf16),
            pltpu.VMEM((many,) + block, bf16),
            pltpu.VMEM((many,) + block, bf16),
            dma((3,)), dma((3,)), dma((high, 3)), dma((high, 3)), dma((many, 3)), dma((many, 3)),
            dma((many, 3)), dma((many, 3)), dma((high, zs, 3)), dma((high, zs, 3)), dma((ys, zs, 3)), dma((ys, zs, 3)),
        ],
        compiler_params=pltpu.CompilerParams(
            collective_id=0, has_side_effects=True, vmem_limit_bytes=60 * MIB),
        name="traction",
    )(ids, ranks, cols, slip, right, coupling, left)


def body(zs, ys, slip_history, frequency_ids, col_clusters, basis_ranks, left_basis, right_basis, coupling):
    ids = frequency_ids.reshape(1, -1)
    slip = jnp.transpose(slip_history, (1, 0, 2))
    right = jnp.transpose(right_basis[0], (0, 1, 3, 2, 4))
    left = jnp.transpose(left_basis[0], (0, 1, 3, 2, 4))
    traction = all_tractions(
        ids, basis_ranks, col_clusters.T, slip, right, coupling[0], left, zs, ys)
    return jnp.transpose(traction, (1, 0, 2))


def solution(mesh):
    ys = max(4 // mesh.shape["group"], 1)
    zs = mesh.shape["freq"] // (2 * ys)
    return jax.shard_map(
        functools.partial(body, zs, ys),
        mesh=mesh,
        in_specs=(
            P("freq", None, "group"),
            P(),
            P(),
            P("freq", "group"),
            P("freq", "group", None, None, None, None),
            P("freq", "group", None, None, None, None),
            P("freq", "group", None, None, None),
        ),
        out_specs=P("freq", None, "group"),
        check_vma=False,
    )
```

```python
import functools
import math

import jax
import jax.numpy as jnp
from jax import lax
from jax.experimental import pallas as pl
from jax.experimental.pallas import tpu as pltpu
from jax.sharding import PartitionSpec as P

STEPS = 512
DAMPING = 0.5
LEAF = 128
CHUNKS = 8
MESH = pl.DeviceIdType.MESH
MIB = 1024 * 1024


def split_f32(x):
    hi = x.astype(jnp.bfloat16)
    lo = (x - hi.astype(jnp.float32)).astype(jnp.bfloat16)
    return hi, lo


def iota(shape, axis):
    return lax.broadcasted_iota(jnp.int32, shape, axis)


def angles_of(frequencies, times):
    phases = (frequencies * times) & (STEPS - 1)
    return phases.astype(jnp.float32) * (2.0 * math.pi / STEPS)


def forward_matrix(ids, first_time, times):
    n = ids.shape[1]
    lanes, rows = CHUNKS * times, n * 2 * CHUNKS
    column = jnp.sum(jnp.where(iota((n, n), 0) == iota((n, n), 1), ids, 0), axis=1, keepdims=True)
    time_ids = iota((n, lanes), 1) % times + first_time
    angles = angles_of(column, time_ids)
    weights = jnp.exp2(time_ids.astype(jnp.float32) * (math.log2(DAMPING) / STEPS))
    table = jnp.concatenate([weights * jnp.cos(angles), -weights * jnp.sin(angles)], axis=0)
    row = iota((rows, 2 * n), 0)
    spread = (iota((rows, 2 * n), 1) == (row // CHUNKS) % 2 * n + row // (2 * CHUNKS)).astype(jnp.bfloat16)
    kept = iota((rows, lanes), 0) % CHUNKS == iota((rows, lanes), 1) // times
    hi, lo = [
        jnp.where(kept, jnp.dot(spread, part, preferred_element_type=jnp.float32), 0.0).astype(jnp.bfloat16)
        for part in split_f32(table)]
    return hi, lo


def inverse_matrix(ids, first_time, times):
    n = ids.shape[1]
    rows, lanes = CHUNKS * times, n * 2 * CHUNKS
    time_ids = iota((rows, n), 0) % times + first_time
    angles = angles_of(ids, time_ids)
    scales = jnp.exp2(time_ids.astype(jnp.float32) * (-math.log2(DAMPING) / STEPS)) / STEPS
    factor = scales * jnp.where((ids == 0) | (ids == STEPS // 2), 1.0, 2.0)
    table = jnp.concatenate([factor * jnp.cos(angles), -factor * jnp.sin(angles)], axis=1)
    lane = iota((2 * n, lanes), 1)
    spread = (iota((2 * n, lanes), 0) == (lane // CHUNKS) % 2 * n + lane // (2 * CHUNKS)).astype(jnp.bfloat16)
    kept = iota((rows, lanes), 1) % CHUNKS == iota((rows, lanes), 0) // times
    return [
        jnp.where(kept, jnp.dot(part, spread, preferred_element_type=jnp.float32), 0.0).astype(jnp.bfloat16)
        for part in split_f32(table)]


def place(zs, ys):
    me = lax.axis_index("freq")
    core = lax.rem(me, 2)
    y = lax.rem(me // 2, ys)
    z = me // (2 * ys)
    return z, y, core


def index_of(z, y, core, ys):
    return (z * ys + y) * 2 + core


def greet(targets):
    barrier = pltpu.get_barrier_semaphore()
    for target in targets:
        pl.semaphore_signal(barrier, inc=1, device_id={"freq": target}, device_id_type=MESH)
    return lambda: pl.semaphore_wait(barrier, len(targets))


def partners(z, y, core, zs, ys):
    targets = [index_of(z, y, 1 - core, ys)]
    targets += [index_of(z, lax.rem(y + s, ys), core, ys) for s in range(1, ys)]
    targets += [index_of(lax.rem(z + s, zs), y, core, ys) for s in range(1, zs)]
    return targets


def scatter_phase(zs, ys, ready, ids, slip_ref, slip_sems, between, acc, send0, recv0, send1, recv1, send2, recv2, sems):
    ss0, rs0, ss1, rs1, ss2, rs2 = sems
    z, y, core = place(zs, ys)
    times, width = slip_ref.shape[1], slip_ref.shape[2] // CHUNKS
    order = list(range(zs // 2, zs // 2 - zs, -1))
    order = [s % zs for s in order if s % zs] + [0]
    table_hi, table_lo = forward_matrix(ids, index_of(z, y, core, ys) * times, times)
    table = jnp.concatenate([table_hi, table_hi, table_lo], axis=1)
    for j in range(3):
        pltpu.make_async_copy(slip_ref.at[j], slip_ref.at[j], slip_sems.at[j]).wait()
        x = jnp.concatenate([slip_ref[j, :, c * width:(c + 1) * width] for c in range(CHUNKS)], axis=0)
        hi, lo = split_f32(x)
        stack = jnp.concatenate([hi, lo, hi], axis=0)
        res = jnp.dot(table, stack, preferred_element_type=jnp.float32)
        res = res.reshape(zs * ys, 2, 2 * CHUNKS, width)
        first, second = res[:, 0], res[:, 1]
        own = jnp.where(core == 0, first, second)
        other = jnp.where(core == 0, second, first)
        acc[:, j] = own
        send0[:, j] = other.astype(jnp.bfloat16)
    ready()
    stage0 = {}
    for s in order:
        at = lax.rem(z + s, zs)
        rows = pl.ds(at * ys, ys)
        stage0[s] = pltpu.make_async_remote_copy(
            src_ref=send0.at[rows], dst_ref=recv0.at[rows], send_sem=ss0.at[s], recv_sem=rs0.at[s],
            device_id={"freq": index_of(z, y, 1 - core, ys)}, device_id_type=MESH)
        stage0[s].start()
    stage1, stage2 = {}, {}
    for s in order:
        at = lax.rem(z + s, zs)
        stage0[s].wait_recv()
        for step in range(1, ys):
            there = lax.rem(y + step, ys)
            block = at * ys + there
            send1[step - 1, at] = (acc[block] + recv0[block].astype(jnp.float32)).astype(jnp.bfloat16)
            stage1[s, step] = pltpu.make_async_remote_copy(
                src_ref=send1.at[step - 1, at], dst_ref=recv1.at[step - 1, at],
                send_sem=ss1.at[step - 1, s], recv_sem=rs1.at[step - 1, s],
                device_id={"freq": index_of(z, there, core, ys)}, device_id_type=MESH)
            stage1[s, step].start()
    for position, s in enumerate(order):
        between(8 * position // zs, 8 * (position + 1) // zs)
        at = lax.rem(z + s, zs)
        block = at * ys + y
        total = acc[block] + recv0[block].astype(jnp.float32)
        for step in range(1, ys):
            stage1[s, step].wait_recv()
            total += recv1[step - 1, at].astype(jnp.float32)
        if s:
            send2[s - 1] = total.astype(jnp.bfloat16)
            stage2[s] = pltpu.make_async_remote_copy(
                src_ref=send2.at[s - 1], dst_ref=recv2.at[s - 1], send_sem=ss2.at[s - 1], recv_sem=rs2.at[s - 1],
                device_id={"freq": index_of(at, y, core, ys)}, device_id_type=MESH)
            stage2[s].start()
    for s in order[:-1]:
        stage2[s].wait_recv()
        total += recv2[s - 1].astype(jnp.float32)
    for copies in (stage0, stage1, stage2):
        for copy in copies.values():
            copy.wait_send()
    return total


def reorder_coupling(coupling_ref, ordered, begin, end):
    groups, blocks = coupling_ref.shape[0] // CHUNKS, coupling_ref.shape[1]

    def step(g, carry):
        rows = pl.ds(pl.multiple_of(g * CHUNKS, CHUNKS), CHUNKS)
        for i in range(blocks):
            found = [coupling_ref[c * groups + g, i].astype(jnp.float32) for c in range(CHUNKS)]
            for q in range(2):
                ordered[q, i, rows, :] = jnp.concatenate([part[q:q + 1] for part in found], axis=0)
        return carry

    lax.fori_loop(begin, end, step, 0)


def operator_phase(spectrum, right_ref, ordered, left_ref, wait_left, rank_row, col_ref, image_ref, coef):
    f32, bf16 = jnp.float32, jnp.bfloat16
    groups = spectrum.shape[2] // LEAF
    rank = right_ref.shape[3]
    clusters = groups * CHUNKS
    blocks = ordered.shape[1]
    chunk_row = lax.broadcasted_iota(jnp.int32, (2 * CHUNKS, 2 * rank), 0) % CHUNKS
    half = CHUNKS // 2
    for g in range(groups):
        lanes = slice(g * LEAF, (g + 1) * LEAF)
        x = jnp.concatenate([spectrum[j, :, lanes] for j in range(3)], axis=1)
        x = jnp.concatenate(split_f32(x), axis=0)
        prod = jnp.zeros((2 * CHUNKS, 2 * rank), f32)
        for h in range(2):
            basis = jnp.concatenate(
                [jnp.concatenate([right_ref[(h * half + c) * groups + g, q, j] for c in range(half) for q in range(2)], axis=0)
                 for j in range(3)], axis=1)
            full = lax.dot_general(x, basis, (((1,), (1,)), ((), ())), preferred_element_type=f32)
            full = full[:2 * CHUNKS] + full[2 * CHUNKS:]
            for c in range(half):
                prod = jnp.where(chunk_row == h * half + c, full[:, c * 2 * rank:(c + 1) * 2 * rank], prod)
        low, high = prod[:CHUNKS], prod[CHUNKS:]
        rows = slice(g * CHUNKS, (g + 1) * CHUNKS)
        coef[0, rows] = low[:, :rank] - high[:, rank:]
        coef[1, rows] = high[:, :rank] + low[:, rank:]
    square = (clusters, clusters)
    cluster_of = iota(square, 0) % CHUNKS * groups + iota(square, 0) // CHUNKS
    ranks = jnp.sum(jnp.where(iota(square, 1) == cluster_of, rank_row, 0), axis=1, keepdims=True)
    kept = iota((clusters, rank), 1) < ranks
    area = rank * rank
    spread = (iota((2 * rank, area), 1) % rank == iota((2 * rank, area), 0) % rank).astype(bf16)
    held = [jnp.concatenate(split_f32(jnp.where(kept, coef[p], 0.0)), axis=1) for p in range(2)]
    sums = [jnp.zeros((clusters, area), f32) for _ in range(2)]
    for i in range(blocks):
        sources = jnp.sum(jnp.where(iota(square, 1) == cluster_of, col_ref[i:i + 1, :], 0), axis=1, keepdims=True)
        source_rows = sources % groups * CHUNKS + sources // groups
        pick = (iota(square, 1) == source_rows).astype(bf16)
        real, imag = [
            jnp.dot(jnp.dot(pick, part, preferred_element_type=f32).astype(bf16), spread, preferred_element_type=f32)
            for part in held]
        low, high = ordered[0, i], ordered[1, i]
        sums[0] += low * real - high * imag
        sums[1] += high * real + low * imag
    gather = (iota((area, rank), 0) // rank == iota((area, rank), 1)).astype(bf16)
    middle = []
    for part in sums:
        hi, lo = split_f32(part)
        short = jnp.dot(hi, gather, preferred_element_type=f32) + jnp.dot(lo, gather, preferred_element_type=f32)
        middle.append(jnp.where(kept, short, 0.0))
    real, imag = middle
    wait_left()
    for g in range(groups):
        rows = slice(g * CHUNKS, (g + 1) * CHUNKS)
        mixed = jnp.concatenate([
            jnp.concatenate([real[rows], -imag[rows]], axis=1),
            jnp.concatenate([imag[rows], real[rows]], axis=1)], axis=0)
        masked = jnp.concatenate([jnp.where(chunk_row == c, mixed, 0.0) for c in range(CHUNKS)], axis=1)
        masked = jnp.concatenate(split_f32(masked), axis=0)
        for j in range(3):
            basis = jnp.concatenate([left_ref[c * groups + g, q, j] for c in range(CHUNKS) for q in range(2)], axis=0)
            out = jnp.dot(masked, basis, preferred_element_type=f32)
            out = out[:2 * CHUNKS] + out[2 * CHUNKS:]
            image_ref[j, :, g * LEAF:(g + 1) * LEAF] = out.astype(bf16)


def gather_phase(zs, ys, image_ref, out_ref, local_sem, meanwhile, finish, sems):
    zsend, zrecv, ysend, yrecv, csend, crecv = sems
    z, y, core = place(zs, ys)
    me = index_of(z, y, core, ys)
    mine = pltpu.make_async_copy(image_ref, out_ref.at[me], local_sem)
    mine.start()
    copies = []

    def send(block, j, source, target, send_sem, recv_sem):
        copy = pltpu.make_async_remote_copy(
            src_ref=source.at[j], dst_ref=out_ref.at[block, j], send_sem=send_sem, recv_sem=recv_sem,
            device_id={"freq": target}, device_id_type=MESH)
        copy.start()
        copies.append(copy)

    other = index_of(z, y, 1 - core, ys)
    far = sorted(range(1, zs), key=lambda s: -min(s, zs - s))
    near = far[::-1]

    def pass_y(block, j, source, s):
        for step in range(1, ys):
            send(block, j, source, index_of(z, lax.rem(y + step, ys), core, ys),
                 ysend.at[step - 1, s, j], yrecv.at[step - 1, s, j])

    def arrived(block, j, recv_sem):
        pltpu.make_async_copy(out_ref.at[block, j], out_ref.at[block, j], recv_sem).wait()

    for j in range(3):
        for s in far:
            send(me, j, image_ref, index_of(lax.rem(z + s, zs), y, core, ys), zsend.at[s - 1, j], zrecv.at[s - 1, j])
        pass_y(me, j, image_ref, 0)
        send(me, j, image_ref, other, csend.at[0, 0, j], crecv.at[0, 0, j])
    meanwhile()

    def from_z(j):
        for s in near:
            block = index_of(lax.rem(z + zs - s, zs), y, core, ys)
            arrived(block, j, zrecv.at[s - 1, j])
            pass_y(block, j, out_ref.at[block], s)
            send(block, j, out_ref.at[block], other, csend.at[0, s, j], crecv.at[0, s, j])

    def from_y(j):
        for s in [0] + near:
            for step in range(1, ys):
                block = index_of(lax.rem(z + zs - s, zs), lax.rem(y + ys - step, ys), core, ys)
                arrived(block, j, yrecv.at[step - 1, s, j])
                send(block, j, out_ref.at[block], other, csend.at[step, s, j], crecv.at[step, s, j])

    def from_core(j):
        for s in [0] + near:
            for step in range(ys):
                block = index_of(lax.rem(z + zs - s, zs), lax.rem(y + ys - step, ys), 1 - core, ys)
                arrived(block, j, crecv.at[step, s, j])
        finish(j)

    from_z(0)
    from_z(1)
    from_y(0)
    from_z(2)
    from_y(1)
    mine.wait()
    from_core(0)
    from_y(2)
    from_core(1)
    from_core(2)
    for copy in copies:
        copy.wait_send()


def traction_kernel(zs, ys, *refs):
    ids_ref, rank_ref, col_ref, slip_hbm, right_hbm, coupling_hbm, left_hbm = refs[:7]
    traction_hbm, images, hi_ref, lo_ref = refs[7:11]
    slip, right, coupling, left, ordered, coef, image, fetch_sems, local_sem = refs[11:20]
    scatter_refs, scatter_sems, gather_sems = refs[20:27], refs[27:33], refs[33:]
    z, y, core = place(zs, ys)
    ready = greet(partners(z, y, core, zs, ys))
    for j in range(3):
        pltpu.make_async_copy(slip_hbm.at[j], slip.at[j], fetch_sems.at[j]).start()
    fetches = [
        pltpu.make_async_copy(source, target, fetch_sems.at[3 + at])
        for at, (source, target) in enumerate([(coupling_hbm, coupling), (right_hbm, right), (left_hbm, left)])]
    for fetch in fetches:
        fetch.start()

    def between(begin, end):
        if begin == 0 and end > 0:
            fetches[0].wait()
        groups = coupling.shape[0] // CHUNKS
        reorder_coupling(coupling, ordered, begin * groups // 8, end * groups // 8)

    spectrum = scatter_phase(zs, ys, ready, ids_ref[...], slip, fetch_sems, between, *scatter_refs, scatter_sems)
    fetches[1].wait()
    operator_phase(spectrum, right, ordered, left, fetches[2].wait, rank_ref[...], col_ref, image, coef)
    times = slip.shape[1]

    def meanwhile():
        hi_ref[...], lo_ref[...] = inverse_matrix(ids_ref[...], index_of(z, y, core, ys) * times, times)

    traction, width = slip, image.shape[2]
    stores = [pltpu.make_async_copy(traction.at[j], traction_hbm.at[j], fetch_sems.at[j]) for j in range(3)]

    def finish(j):
        x = images[:, j].reshape(-1, width)
        res = jnp.dot(hi_ref[...], x, preferred_element_type=jnp.float32)
        res += jnp.dot(lo_ref[...], x, preferred_element_type=jnp.float32)
        for c in range(CHUNKS):
            traction[j, :, c * width:(c + 1) * width] = res[c * times:(c + 1) * times]
        stores[j].start()

    gather_phase(zs, ys, image, images, local_sem, meanwhile, finish, gather_sems)
    for store in stores:
        store.wait()


def all_tractions(ids, ranks, cols, slip, right, coupling, left, zs, ys):
    times, n = slip.shape[1], zs * ys * 2
    clusters, rank, blocks = right.shape[0], right.shape[3], coupling.shape[1]
    block = (3, 2 * CHUNKS, slip.shape[2] // CHUNKS)
    f32, bf16 = jnp.float32, jnp.bfloat16
    high, many = max(ys - 1, 1), max(zs - 1, 1)
    middle = (high, zs) if ys > 1 else (1, 1)
    vmem, hbm = pl.BlockSpec(memory_space=pltpu.VMEM), pl.BlockSpec(memory_space=pl.ANY)
    matrix = pltpu.VMEM((CHUNKS * times, n * 2 * CHUNKS), bf16)
    dma = pltpu.SemaphoreType.DMA
    return pl.pallas_call(
        functools.partial(traction_kernel, zs, ys),
        out_shape=jax.ShapeDtypeStruct(slip.shape, f32),
        in_specs=[vmem, vmem, vmem, hbm, hbm, hbm, hbm],
        out_specs=hbm,
        scratch_shapes=[
            pltpu.VMEM((n,) + block, bf16),
            matrix,
            matrix,
            pltpu.VMEM(slip.shape, f32),
            pltpu.VMEM(right.shape, bf16),
            pltpu.VMEM(coupling.shape, bf16),
            pltpu.VMEM(left.shape, bf16),
            pltpu.VMEM((2, blocks, clusters, rank * rank), f32),
            pltpu.VMEM((2, clusters, rank), f32),
            pltpu.VMEM(block, bf16),
            dma((6,)),
            dma,
            pltpu.VMEM((zs * ys,) + block, f32),
            pltpu.VMEM((zs * ys,) + block, bf16),
            pltpu.VMEM((zs * ys,) + block, bf16),
            pltpu.VMEM(middle + block, bf16),
            pltpu.VMEM(middle + block, bf16),
            pltpu.VMEM((many,) + block, bf16),
            pltpu.VMEM((many,) + block, bf16),
            dma((zs,)), dma((zs,)), dma((high, zs)), dma((high, zs)), dma((many,)), dma((many,)),
            dma((many, 3)), dma((many, 3)), dma((high, zs, 3)), dma((high, zs, 3)), dma((ys, zs, 3)), dma((ys, zs, 3)),
        ],
        compiler_params=pltpu.CompilerParams(
            collective_id=0, has_side_effects=True, vmem_limit_bytes=60 * MIB),
        name="traction",
    )(ids, ranks, cols, slip, right, coupling, left)


def body(zs, ys, slip_history, frequency_ids, col_clusters, basis_ranks, left_basis, right_basis, coupling):
    ids = frequency_ids.reshape(1, -1)
    slip = jnp.transpose(slip_history, (1, 0, 2))
    right = jnp.transpose(right_basis[0], (0, 1, 3, 2, 4))
    left = jnp.transpose(left_basis[0], (0, 1, 3, 2, 4))
    traction = all_tractions(
        ids, basis_ranks, col_clusters.T, slip, right, coupling[0], left, zs, ys)
    return jnp.transpose(traction, (1, 0, 2))


def solution(mesh):
    ys = max(4 // mesh.shape["group"], 1)
    zs = mesh.shape["freq"] // (2 * ys)
    return jax.shard_map(
        functools.partial(body, zs, ys),
        mesh=mesh,
        in_specs=(
            P("freq", None, "group"),
            P(),
            P(),
            P("freq", "group"),
            P("freq", "group", None, None, None, None),
            P("freq", "group", None, None, None, None),
            P("freq", "group", None, None, None),
        ),
        out_specs=P("freq", None, "group"),
        check_vma=False,
    )
```
